512 devices in a mesh: ka: 128 (over y, z, core), pair: 4 (over x).
Axes of the slice: x: 4, y: 8, z: 8, core: 2. Of those that a mesh axis runs over, the one named last changes fastest.
Arguments:
- kkr_matrix: bfloat16 [512, 2, 256, 256], P('ka'), may hold values from -0.125 to 0.125
- kpoint_grid: int32 [512, 3], P('ka'), may hold values from 0 to 15
- lattice: int32 [8, 3], replicated, may hold values from -3 to 3, as said below
- delta_t: bfloat16 [4, 2, 256, 256], replicated, may hold values from -0.25 to 0.25
- pair_count: int32 [128], replicated, may hold values from 1 to 8, as said below
- pair_route: int32 [128, 8], replicated, may hold values from 0 to 7
- species: int32 [128, 8], replicated, may hold values from 0 to 3
Outputs:
- host_blocks: float32 [2048, 512], P('ka', 'pair')
- cluster_blocks: bfloat16 [1024, 256, 512], P('ka', None, 'pair')
The draws below stay inside these ranges and needn't reach their ends.
Inputs may be any that keep to these rules, and one draw needn't show every extreme that they name: Distinct lattice vectors, each component from -3 to 3. `pair_count`: every owner holds at least one pair; some owner, drawn from the seed, fills all 8 slots; slots at or past an owner's count are ignored.
All inputs are finite; a program needn't handle non-finite values.
Results may differ from the reference program's by a relative error of at most 0.0049.
Values may be sent and summed in bfloat16 or wider, within the bound.
No kernel may reach another device: no remote copies, remote signals or barrier semaphores. Data moves between devices by JAX's collectives and lax.ppermute only.
A program may use at most 64 MiB of HBM per device.

```python
import math
import jax
import jax.numpy as jnp
from jax import lax

B = 256
K_DEV = 4
NR = 8
SLOTS = 8
SPECIES = 4
ITERS = 6
KG = 16
COLS = 64
KPTS = 512
OWNERS = 128
N_KA = 128
N_PAIR = 4


def draw_lattice(key, part):
    key = jax.random.fold_in(key, 11)
    first_key, second_key = jax.random.split(key)
    others = (jax.random.permutation(first_key, 341)[:NR - 2] + 1).astype(jnp.int32)
    corners = jnp.array([0, 342], dtype=jnp.int32)
    picked = jnp.concatenate([corners, others]).astype(jnp.int32)
    shuffle = jax.random.permutation(second_key, NR).astype(jnp.int32)
    picked = jnp.take(picked, shuffle, axis=0).astype(jnp.int32)
    first_comp = picked // 49 - 3
    second_comp = picked // 7 % 7 - 3
    third_comp = picked % 7 - 3
    return jnp.stack([first_comp, second_comp, third_comp], axis=1).astype(jnp.int32)


def draw_pair_count(key, part):
    key = jax.random.fold_in(key, 23)
    first_key, second_key = jax.random.split(key)
    counts = jax.random.randint(first_key, (OWNERS,), 1, SLOTS // 2 + 1, dtype=jnp.int32)
    busiest = jax.random.randint(second_key, (), 0, OWNERS, dtype=jnp.int32)
    return counts.at[busiest].set(SLOTS).astype(jnp.int32)


def touch_ends(values, key, low, top_value):
    extent = values.shape
    spot = [jax.random.randint(jax.random.fold_in(key, axis), (), 0, extent[axis]) for axis in range(len(extent))]
    values = values.at[tuple(spot)].set(low)
    longest = extent.index(max(extent))
    spot[longest] = (spot[longest] + 1) % extent[longest]
    return values.at[tuple(spot)].set(top_value)


def block_scale(key, extent, pieces, least, top_value):
    loudness, own = 1.0, jax.random.fold_in(key, 6)
    for axis_at, shards_of in pieces:
        draws = jnp.exp(jax.random.uniform(jax.random.fold_in(own, axis_at), (shards_of,), jnp.float32, least / len(pieces), top_value / len(pieces)))
        loudness = loudness * jnp.repeat(draws, extent[axis_at] // shards_of).reshape([-1 if axis == axis_at else 1 for axis in range(len(extent))])
    return loudness


def scatter_about(stream_key, extent, deviation, limit, cuts=(), kind=jnp.bfloat16):
    loudness = block_scale(stream_key, extent, cuts, -0.22, 0.18) if cuts else 1.0
    values = jax.random.normal(stream_key, extent, jnp.float32) * deviation * loudness
    return jnp.minimum(jnp.maximum(values, -limit), limit).astype(kind)


def setup_inputs(seed: int = 0) -> dict:
    seeds = jax.random.split(jax.random.key(seed), 8)
    return {
        "kkr_matrix": scatter_about(seeds[0], (KPTS, 2, B, B), (0.35 / B ** 0.5), 0.125, ((0, 128),)),
        "kpoint_grid": touch_ends(jax.random.randint(seeds[1], (KPTS, 3), 0, KG), jax.random.fold_in(seeds[1], 1), 0, KG - 1).astype(jnp.int32),
        "lattice": draw_lattice(jax.random.fold_in(seeds[7], 71), 0),
        "delta_t": scatter_about(seeds[3], (SPECIES, 2, B, B), (2 * B) ** -0.5, 0.25),
        "pair_count": draw_pair_count(jax.random.fold_in(seeds[7], 71), 0),
        "pair_route": touch_ends(jax.random.randint(seeds[5], (OWNERS, SLOTS), 0, NR), jax.random.fold_in(seeds[5], 1), 0, NR - 1).astype(jnp.int32),
        "species": touch_ends(jax.random.randint(seeds[6], (OWNERS, SLOTS), 0, SPECIES), jax.random.fold_in(seeds[6], 1), 0, SPECIES - 1).astype(jnp.int32),
    }


PRECISE = lax.Precision.HIGHEST

def phases(kpoint_grid, lattice):
    turn_index = jnp.mod(jnp.dot(kpoint_grid, lattice.T), KG).astype(jnp.float32)
    angles = turn_index * (2.0 * math.pi / KG)
    return (jnp.cos(angles), jnp.sin(angles))

def reference(kkr_matrix, kpoint_grid, lattice, delta_t, pair_count, pair_route, species):
    cosine, sine_part = phases(kpoint_grid, lattice)

    def accumulate(totals, inputs):
        matrix, cos_row, sin_row = inputs
        real_kkr = matrix[0].astype(jnp.float32)
        imag_kkr = matrix[1].astype(jnp.float32)
        real_x, imag_x = (real_kkr, imag_kkr)
        for iteration in range(ITERS - 1):
            new_real = real_kkr + jnp.dot(real_kkr, real_x, precision=PRECISE) - jnp.dot(imag_kkr, imag_x, precision=PRECISE)
            new_imag = imag_kkr + jnp.dot(real_kkr, imag_x, precision=PRECISE) + jnp.dot(imag_kkr, real_x, precision=PRECISE)
            real_x, imag_x = (new_real, new_imag)
        sum_real, sum_imag = totals
        sum_real = sum_real + cos_row[:, None, None] * real_x[None] - sin_row[:, None, None] * imag_x[None]
        sum_imag = sum_imag + cos_row[:, None, None] * imag_x[None] + sin_row[:, None, None] * real_x[None]
        return ((sum_real, sum_imag), None)
    zeros = jnp.zeros((NR, B, B), jnp.float32)
    (sum_real, sum_imag), unused = lax.scan(accumulate, (zeros, zeros), (kkr_matrix, cosine, sine_part))
    weight_scale = math.sqrt(B / (K_DEV * N_KA))
    stacked = jnp.stack([sum_real, sum_imag], axis=0) * weight_scale
    host_blocks = stacked.reshape(2, NR, B, N_PAIR, COLS).transpose(2, 1, 3, 0, 4).reshape(B * NR, 2 * B)
    rounded_rows = host_blocks.astype(jnp.bfloat16).reshape(B, NR, N_PAIR, 2, COLS)
    alive_mask = jnp.arange(SLOTS)[None, :] < pair_count[:, None]

    def embed(inputs):
        route_index, species_index, alive_flag = inputs
        row_block = rounded_rows[:, route_index]
        real_g = row_block[:, :, 0, :].reshape(B, B)
        imag_g = row_block[:, :, 1, :].reshape(B, B)
        left_side = jnp.concatenate([real_g, imag_g], axis=1).astype(jnp.float32)
        real_t = delta_t[species_index, 0]
        imag_t = delta_t[species_index, 1]
        right_side = jnp.concatenate([jnp.concatenate([real_t, imag_t], 1), jnp.concatenate([-imag_t, real_t], 1)], 0).astype(jnp.float32)
        product = jnp.dot(left_side, right_side, preferred_element_type=jnp.float32)
        product = jnp.where(alive_flag, product, jnp.zeros_like(product))
        result = product.reshape(B, 2, N_PAIR, COLS).transpose(0, 2, 1, 3).reshape(B, 2 * B)
        return result.astype(jnp.bfloat16)
    cluster_blocks = lax.map(embed, (pair_route.reshape(-1), species.reshape(-1), alive_mask.reshape(-1)))
    return (host_blocks, cluster_blocks)
```

```python
import functools
import math

import jax
import jax.numpy as jnp
import numpy as np
from jax import lax
from jax.experimental import pallas as pl
from jax.experimental.pallas import tpu as pltpu
from jax.sharding import Mesh
from jax.sharding import PartitionSpec as P

ITERS = 6
KG = 16
LANES = 128
CHIPS = ("y", "z")
CORES = ("c", "pair")
F32 = jnp.float32
BF16 = jnp.bfloat16


def dot(a, b):
    return jnp.dot(a, b, preferred_element_type=F32)


def turn_tables():
    angles = np.arange(KG) * (2.0 * math.pi / KG)
    tables = []
    for values in (np.cos(angles), np.sin(angles)):
        values = values.astype(np.float32)
        high = values.astype(jnp.bfloat16).astype(np.float32)
        tables += [high, (values - high).astype(jnp.bfloat16).astype(np.float32)]
    return tables


def solve_kernel(spot, grid, lattice, matrix, out, wide):
    kpoints, _, order, _ = matrix.shape
    own = order // 4
    chunk = out.shape[0] // own
    row = lax.broadcasted_iota(jnp.int32, (own, order), 0)
    col = lax.broadcasted_iota(jnp.int32, (own, order), 1)
    pick = jnp.where(col == row * 4 + spot[0], 1.0, 0.0).astype(BF16)
    first = [[dot(pick, matrix[k, part]) for part in range(2)] for k in range(kpoints)]
    now = [list(pair) for pair in first]
    for step in range(ITERS - 1):
        for k in range(kpoints):
            re, im = now[k]
            re_high, im_high = re.astype(BF16), im.astype(BF16)
            parts = [re_high, im_high]
            if step > 0:
                parts.append((re - re_high.astype(F32)).astype(BF16))
                parts.append((im - im_high.astype(F32)).astype(BF16))
            left = jnp.concatenate(parts, axis=0)
            u = dot(left, matrix[k, 0])
            v = dot(left, matrix[k, 1])
            if step > 0:
                u = u[: 2 * own] + u[2 * own :]
                v = v[: 2 * own] + v[2 * own :]
            now[k] = [
                first[k][0] + u[:own] - v[own:],
                first[k][1] + v[:own] + u[own:],
            ]
    for k in range(kpoints):
        for part in range(2):
            for half in range(order // LANES):
                place = (k * 2 + part) * (order // LANES) + half
                wide[pl.ds(place, own, stride=chunk), :] = now[k][part][
                    :, half * LANES : (half + 1) * LANES
                ]
    vectors = lattice.shape[0]
    lane = lax.broadcasted_iota(jnp.int32, (8, LANES), 1)
    turn = jnp.zeros((8, LANES), jnp.int32)
    for r in range(vectors):
        for k in range(kpoints):
            m = (
                grid[k, 0] * lattice[r, 0]
                + grid[k, 1] * lattice[r, 1]
                + grid[k, 2] * lattice[r, 2]
            ) & (KG - 1)
            here = ((lane // (4 * vectors)) == k) & ((lane & (vectors - 1)) == r)
            turn = jnp.where(here, m, turn)
    kind = (lane // vectors) & 3
    phase = jnp.zeros((8, LANES), F32)
    for which, table in enumerate(turn_tables()):
        for m in range(KG):
            phase = jnp.where((kind == which) & (turn == m), float(table[m]), phase)
    phase = jnp.broadcast_to(phase[:1], (own, LANES))
    wide[pl.ds(chunk - 2, own, stride=chunk), :] = phase
    wide[pl.ds(chunk - 1, own, stride=chunk), :] = jnp.zeros((own, LANES), F32)
    out[...] = wide[...].astype(BF16)


def phase_kernel(kpoints, vectors, rows, out, wide):
    chunk = 2 + 4 * kpoints
    sources = rows.shape[0] // chunk
    wide[...] = rows[...].astype(F32)
    info = wide[pl.ds(chunk - 2, sources, stride=chunk), :]
    info = jnp.transpose(info).astype(BF16)
    total = jnp.zeros((4 * vectors, 4 * LANES), F32)
    for k in range(kpoints):
        block = [wide[pl.ds(k * 4 + q, sources, stride=chunk), :] for q in range(4)]
        block = jnp.concatenate(block, axis=1).astype(BF16)
        total = total + dot(info[k * 4 * vectors : (k + 1) * 4 * vectors], block)
    cosine = total[:vectors] + total[vectors : 2 * vectors]
    sine = total[2 * vectors : 3 * vectors] + total[3 * vectors :]
    half = 2 * LANES
    re = cosine[:, :half] - sine[:, half:]
    im = cosine[:, half:] + sine[:, :half]
    both = jnp.concatenate([re, im], axis=1)
    out[...] = jnp.broadcast_to(both[None], out.shape)


def coupling_kernel(spot, delta, out):
    kinds, _, order, _ = delta.shape
    row = lax.broadcasted_iota(jnp.int32, (order, LANES), 0)
    col = lax.broadcasted_iota(jnp.int32, (order, LANES), 1)
    half = LANES // 2
    left = ((col < half) & (row == spot[0] * half + col)).astype(F32).astype(BF16)
    right = ((col >= half) & (row == spot[0] * half + col - half)).astype(F32).astype(BF16)
    for s in range(kinds):
        re, im = delta[s, 0], delta[s, 1]
        out[:order, s * LANES : (s + 1) * LANES] = (dot(re, left) + dot(im, right)).astype(BF16)
        out[order:, s * LANES : (s + 1) * LANES] = (dot(re, right) - dot(im, left)).astype(BF16)


def product_kernel(scale, spot, parts, coupling, chosen, host, out, wide, sums):
    vectors = parts.shape[1]
    order = parts.shape[2] // 2
    half = LANES // 2
    for q in range(4):
        sums[q * vectors : (q + 1) * vectors, :] = (parts[q] + parts[4 + q]) * scale
    own = pl.multiple_of(spot[1] * (2 * vectors), 2 * vectors)
    at = pl.multiple_of((spot[0] // 2) * LANES, LANES)
    re = sums[pl.ds(own, 2 * vectors), pl.ds(at, LANES)]
    im = sums[pl.ds(own, 2 * vectors), pl.ds(order + at, LANES)]
    lane = lax.broadcasted_iota(jnp.int32, re.shape, 1)
    odd = (spot[0] & 1) == 1
    re = jnp.where(odd, pltpu.roll(re, half, 1), re)
    im = jnp.where(odd, im, pltpu.roll(im, half, 1))
    host[...] = jnp.where(lane < half, re, im)
    product = dot(sums[...].astype(BF16), coupling[...])
    kinds = coupling.shape[1] // LANES
    table = jnp.concatenate(
        [
            jnp.concatenate(
                [
                    product[q * vectors : (q + 1) * vectors, s * LANES : (s + 1) * LANES]
                    for q in range(4)
                ],
                axis=1,
            )
            for s in range(kinds)
        ],
        axis=0,
    ).astype(BF16)
    picked = dot(chosen[...], table)
    for q in range(4):
        wide[pl.ds(q, picked.shape[0], stride=4), :] = picked[:, q * LANES : (q + 1) * LANES]
    out[...] = wide[...].astype(BF16)


VMEM = pl.BlockSpec(memory_space=pltpu.VMEM)
SMEM = pl.BlockSpec(memory_space=pltpu.SMEM)


def params():
    return pltpu.CompilerParams(vmem_limit_bytes=32 * 1024 * 1024)


def per_device(kkr_matrix, kpoint_grid, lattice, delta_t, pair_count, pair_route, species):
    chips = lax.axis_size(CHIPS)
    cores = lax.axis_size(CORES)
    pair = lax.axis_index("pair")
    core = lax.axis_index("c")
    spot = jnp.stack([pair, core]).astype(jnp.int32)
    order = kkr_matrix.shape[2]
    kpoints = kkr_matrix.shape[0]
    vectors = lattice.shape[0]
    slots = pair_route.shape[1]
    kinds = delta_t.shape[0]
    scale = math.sqrt(order / (kpoints * chips * lax.axis_size("c")))
    chunk = 4 * kpoints + 2
    length = chips * chunk

    outgoing = pl.pallas_call(
        solve_kernel,
        out_shape=jax.ShapeDtypeStruct((length, LANES), BF16),
        in_specs=[SMEM, SMEM, SMEM, VMEM],
        out_specs=VMEM,
        scratch_shapes=[pltpu.VMEM((length, LANES), F32)],
        compiler_params=params(),
        name="solve",
    )(spot, kpoint_grid, lattice, kkr_matrix)
    outgoing = outgoing.reshape(chips, chunk // 2, 2, LANES)
    arrived = lax.all_to_all(outgoing, CHIPS, split_axis=0, concat_axis=0, tiled=True)

    coupling = pl.pallas_call(
        coupling_kernel,
        out_shape=jax.ShapeDtypeStruct((2 * order, kinds * LANES), BF16),
        in_specs=[SMEM, VMEM],
        out_specs=VMEM,
        compiler_params=params(),
        cost_estimate=pl.CostEstimate(
            flops=16 * kinds * order * order * LANES, bytes_accessed=2 << 20, transcendentals=0
        ),
        name="coupling",
    )(spot, delta_t)
    alive = jnp.arange(slots)[None, :] < pair_count[:, None]
    combo = jnp.where(alive, species * vectors + pair_route, -1)
    combo = lax.dynamic_index_in_dim(combo.reshape(chips, 2, slots), core, 1, keepdims=False)
    chosen = (combo.reshape(-1, 1) == jnp.arange(kinds * vectors)[None, :]).astype(BF16)

    parts = pl.pallas_call(
        functools.partial(phase_kernel, kpoints, vectors),
        out_shape=jax.ShapeDtypeStruct((cores, vectors, 2 * order), F32),
        in_specs=[VMEM],
        out_specs=VMEM,
        scratch_shapes=[pltpu.VMEM((length, LANES), F32)],
        compiler_params=params(),
        name="phase_sum",
    )(arrived.reshape(length, LANES))
    parts = lax.all_to_all(parts, CORES, split_axis=0, concat_axis=0, tiled=True)

    host_rows, sent = pl.pallas_call(
        functools.partial(product_kernel, scale),
        out_shape=(
            jax.ShapeDtypeStruct((2 * vectors, LANES), F32),
            jax.ShapeDtypeStruct((chips * slots * 4, LANES), BF16),
        ),
        in_specs=[SMEM, VMEM, VMEM, VMEM],
        out_specs=(VMEM, VMEM),
        scratch_shapes=[
            pltpu.VMEM((chips * slots * 4, LANES), F32),
            pltpu.VMEM((4 * vectors, 2 * order), F32),
        ],
        compiler_params=params(),
        name="product",
    )(spot, parts, coupling, chosen)
    sent = sent.reshape(chips, slots * 4, LANES)
    got = lax.all_to_all(sent, CHIPS, split_axis=0, concat_axis=0, tiled=True)
    cluster = got.reshape(chips, slots, 4, LANES).transpose(1, 0, 2, 3)
    return (host_rows, cluster.reshape(slots, order, LANES))


def solution(mesh):
    fine = Mesh(mesh.devices.reshape(8, 8, 2, 4), ("y", "z", "c", "pair"))
    ka = ("y", "z", "c")
    in_specs = (P(ka, None, None, None), P(ka, None), P(), P(), P(), P(), P())
    out_specs = (P(ka, "pair"), P(ka, None, "pair"))
    return jax.shard_map(
        per_device, mesh=fine, in_specs=in_specs, out_specs=out_specs, check_vma=False
    )
```

```python
import functools
import math

import jax
import jax.numpy as jnp
import numpy as np
from jax import lax
from jax.experimental import pallas as pl
from jax.experimental.pallas import tpu as pltpu
from jax.sharding import Mesh
from jax.sharding import PartitionSpec as P

ITERS = 6
KG = 16
LANES = 128
CHIPS = ("y", "z")
CORES = ("c", "pair")
F32 = jnp.float32
BF16 = jnp.bfloat16


def dot(a, b):
    return jnp.dot(a, b, preferred_element_type=F32)


def turn_tables():
    angles = np.arange(KG) * (2.0 * math.pi / KG)
    tables = []
    for values in (np.cos(angles), np.sin(angles)):
        values = values.astype(np.float32)
        high = values.astype(jnp.bfloat16).astype(np.float32)
        tables += [high, (values - high).astype(jnp.bfloat16).astype(np.float32)]
    return tables


def solve_kernel(grid, lattice, matrix, out, wide):
    kpoints, _, order, _ = matrix.shape
    own = order // 4
    chunk = out.shape[0] // own
    row = lax.broadcasted_iota(jnp.int32, (own, order), 0)
    col = lax.broadcasted_iota(jnp.int32, (own, order), 1)
    pick = jnp.where(col == row * 4 + lax.axis_index("pair"), 1.0, 0.0).astype(BF16)
    first = [[dot(pick, matrix[k, part]) for part in range(2)] for k in range(kpoints)]
    now = [list(pair) for pair in first]
    for step in range(ITERS - 1):
        for k in range(kpoints):
            re, im = now[k]
            re_high, im_high = re.astype(BF16), im.astype(BF16)
            parts = [re_high, im_high]
            if step > 0:
                parts.append((re - re_high.astype(F32)).astype(BF16))
                parts.append((im - im_high.astype(F32)).astype(BF16))
            left = jnp.concatenate(parts, axis=0)
            u = dot(left, matrix[k, 0])
            v = dot(left, matrix[k, 1])
            if step > 0:
                u = u[: 2 * own] + u[2 * own :]
                v = v[: 2 * own] + v[2 * own :]
            now[k] = [
                first[k][0] + u[:own] - v[own:],
                first[k][1] + v[:own] + u[own:],
            ]
    for k in range(kpoints):
        for part in range(2):
            for half in range(order // LANES):
                place = (k * 2 + part) * (order // LANES) + half
                wide[pl.ds(place, own, stride=chunk), :] = now[k][part][
                    :, half * LANES : (half + 1) * LANES
                ]
    vectors = lattice.shape[1]
    lane = lax.broadcasted_iota(jnp.int32, (8, LANES), 1)
    turn = jnp.zeros((8, LANES), jnp.int32)
    for r in range(vectors):
        for k in range(kpoints):
            m = (
                grid[k, 0] * lattice[0, r]
                + grid[k, 1] * lattice[1, r]
                + grid[k, 2] * lattice[2, r]
            ) & (KG - 1)
            here = ((lane // (4 * vectors)) == k) & ((lane & (vectors - 1)) == r)
            turn = jnp.where(here, m, turn)
    kind = (lane // vectors) & 3
    phase = jnp.zeros((8, LANES), F32)
    for which, table in enumerate(turn_tables()):
        for m in range(KG):
            phase = jnp.where((kind == which) & (turn == m), float(table[m]), phase)
    phase = jnp.broadcast_to(phase[:1], (own, LANES))
    wide[pl.ds(chunk - 2, own, stride=chunk), :] = phase
    wide[pl.ds(chunk - 1, own, stride=chunk), :] = jnp.zeros((own, LANES), F32)
    out[...] = wide[...].astype(BF16)


def phase_kernel(kpoints, vectors, rows, out, wide):
    chunk = 2 + 4 * kpoints
    sources = rows.shape[0] // chunk
    wide[...] = rows[...].astype(F32)
    info = wide[pl.ds(chunk - 2, sources, stride=chunk), :]
    info = jnp.transpose(info).astype(BF16)
    total = jnp.zeros((4 * vectors, 4 * LANES), F32)
    for k in range(kpoints):
        block = [wide[pl.ds(k * 4 + q, sources, stride=chunk), :] for q in range(4)]
        block = jnp.concatenate(block, axis=1).astype(BF16)
        total = total + dot(info[k * 4 * vectors : (k + 1) * 4 * vectors], block)
    cosine = total[:vectors] + total[vectors : 2 * vectors]
    sine = total[2 * vectors : 3 * vectors] + total[3 * vectors :]
    half = 2 * LANES
    re = cosine[:, :half] - sine[:, half:]
    im = cosine[:, half:] + sine[:, :half]
    both = jnp.concatenate([re, im], axis=1)
    out[...] = jnp.broadcast_to(both[None], out.shape)


def product_kernel(scale, parts, delta, route, species, count, host, out, wide, sums):
    vectors = parts.shape[1]
    kinds, _, order, _ = delta.shape
    slots, owners = route.shape
    pair, core = lax.axis_index("pair"), lax.axis_index("c")
    half = LANES // 2
    for q in range(4):
        sums[q * vectors : (q + 1) * vectors, :] = (parts[q] + parts[4 + q]) * scale
    odd = (pair & 1) == 1
    lane = lax.broadcasted_iota(jnp.int32, (1, LANES), 1)

    def window(re, im):
        re = jnp.where(odd, pltpu.roll(re, half, 1), re)
        im = jnp.where(odd, im, pltpu.roll(im, half, 1))
        return jnp.where(lane < half, re, im)

    own = pl.multiple_of(core * (2 * vectors), 2 * vectors)
    at = pl.multiple_of((pair // 2) * LANES, LANES)
    host[...] = window(
        sums[pl.ds(own, 2 * vectors), pl.ds(at, LANES)],
        sums[pl.ds(own, 2 * vectors), pl.ds(order + at, LANES)],
    )
    rows = 4 * vectors
    left = jnp.concatenate([sums[:, :order], sums[:, order:]], axis=0).astype(BF16)
    table = []
    for s in range(kinds):
        u = dot(left, delta[s, 0])
        v = dot(left, delta[s, 1])
        re = u[:rows] - v[rows:]
        im = v[:rows] + u[rows:]
        re = jnp.where(pair >= 2, re[:, LANES:], re[:, :LANES])
        im = jnp.where(pair >= 2, im[:, LANES:], im[:, :LANES])
        product = window(re, im)
        table.append(
            jnp.concatenate([product[q * vectors : (q + 1) * vectors] for q in range(4)], axis=1)
        )
    table = jnp.concatenate(table, axis=0).astype(BF16)
    alive = lax.broadcasted_iota(jnp.int32, (slots, owners), 0) < count[...]
    combo = jnp.where(alive, species[...] * vectors + route[...], kinds * vectors)
    combo = jnp.transpose(combo.astype(F32)).astype(BF16)
    chips = owners // 2
    row = lax.broadcasted_iota(jnp.int32, (chips, owners), 0)
    col = lax.broadcasted_iota(jnp.int32, (chips, owners), 1)
    combo = dot(jnp.where(col == row * 2 + core, 1.0, 0.0).astype(BF16), combo)
    kind = lax.broadcasted_iota(jnp.int32, (chips, kinds * vectors), 1).astype(F32)
    chosen = [
        jnp.where(jnp.broadcast_to(combo[:, t : t + 1], kind.shape) == kind, 1.0, 0.0)
        for t in range(slots)
    ]
    chosen = jnp.concatenate(chosen, axis=0).astype(BF16)
    picked = dot(chosen, table)
    for t in range(slots):
        for q in range(4):
            wide[pl.ds(t * 4 + q, chips, stride=4 * slots), :] = picked[
                t * chips : (t + 1) * chips, q * LANES : (q + 1) * LANES
            ]
    out[...] = wide[...].astype(BF16)


def place_kernel(got, out, sems):
    copies = [
        pltpu.make_async_copy(got.at[:, t], out.at[t], sems.at[t]) for t in range(out.shape[0])
    ]
    for copy in copies:
        copy.start()
    for copy in copies:
        copy.wait()


VMEM = pl.BlockSpec(memory_space=pltpu.VMEM)
SMEM = pl.BlockSpec(memory_space=pltpu.SMEM)
HBM = pl.BlockSpec(memory_space=pltpu.HBM)


def params():
    return pltpu.CompilerParams(vmem_limit_bytes=32 * 1024 * 1024)


def per_device(kkr_matrix, kpoint_grid, lattice, delta_t, pair_count, pair_route, species):
    chips = lax.axis_size(CHIPS)
    cores = lax.axis_size(CORES)
    order = kkr_matrix.shape[2]
    kpoints = kkr_matrix.shape[0]
    vectors = lattice.shape[0]
    slots = pair_route.shape[1]
    scale = math.sqrt(order / (kpoints * chips * lax.axis_size("c")))
    chunk = 4 * kpoints + 2
    length = chips * chunk

    outgoing = pl.pallas_call(
        solve_kernel,
        out_shape=jax.ShapeDtypeStruct((length, LANES), BF16),
        in_specs=[SMEM, SMEM, VMEM],
        out_specs=VMEM,
        scratch_shapes=[pltpu.VMEM((length, LANES), F32)],
        compiler_params=params(),
        name="solve",
    )(kpoint_grid, lattice.T, kkr_matrix)
    outgoing = outgoing.reshape(chips, chunk // 2, 2, LANES)
    arrived = lax.all_to_all(outgoing, CHIPS, split_axis=0, concat_axis=0, tiled=True)

    parts = pl.pallas_call(
        functools.partial(phase_kernel, kpoints, vectors),
        out_shape=jax.ShapeDtypeStruct((cores, vectors, 2 * order), F32),
        in_specs=[VMEM],
        out_specs=VMEM,
        scratch_shapes=[pltpu.VMEM((length, LANES), F32)],
        compiler_params=params(),
        name="phase_sum",
    )(arrived.reshape(length, LANES))
    parts = lax.all_to_all(parts, CORES, split_axis=0, concat_axis=0, tiled=True)

    host_rows, sent = pl.pallas_call(
        functools.partial(product_kernel, scale),
        out_shape=(
            jax.ShapeDtypeStruct((2 * vectors, LANES), F32),
            jax.ShapeDtypeStruct((chips * slots * 4, LANES), BF16),
        ),
        in_specs=[VMEM, VMEM, VMEM, VMEM, VMEM],
        out_specs=(VMEM, VMEM),
        scratch_shapes=[
            pltpu.VMEM((chips * slots * 4, LANES), F32),
            pltpu.VMEM((4 * vectors, 2 * order), F32),
        ],
        compiler_params=params(),
        name="product",
    )(parts, delta_t, pair_route.T, species.T, pair_count[None])
    sent = sent.reshape(chips, slots * 4, LANES)
    got = lax.all_to_all(sent, CHIPS, split_axis=0, concat_axis=0, tiled=True)
    cluster = pl.pallas_call(
        place_kernel,
        out_shape=jax.ShapeDtypeStruct((slots, chips, 4, LANES), BF16),
        in_specs=[VMEM],
        out_specs=HBM,
        scratch_shapes=[pltpu.SemaphoreType.DMA((slots,))],
        compiler_params=params(),
        name="place",
    )(got.reshape(chips, slots, 4, LANES))
    return (host_rows, cluster.reshape(slots, order, LANES))


def solution(mesh):
    fine = Mesh(mesh.devices.reshape(8, 8, 2, 4), ("y", "z", "c", "pair"))
    ka = ("y", "z", "c")
    in_specs = (P(ka, None, None, None), P(ka, None), P(), P(), P(), P(), P())
    out_specs = (P(ka, "pair"), P(ka, None, "pair"))
    return jax.shard_map(
        per_device, mesh=fine, in_specs=in_specs, out_specs=out_specs, check_vma=False
    )
```

```python
import functools
import math

import jax
import jax.numpy as jnp
import numpy as np
from jax import lax
from jax.experimental import pallas as pl
from jax.experimental.pallas import tpu as pltpu
from jax.sharding import Mesh
from jax.sharding import PartitionSpec as P

ITERS = 6
KG = 16
LANES = 128
CHIPS = ("y", "z")
CORES = ("c", "pair")
F32 = jnp.float32
BF16 = jnp.bfloat16


def dot(a, b):
    return jnp.dot(a, b, preferred_element_type=F32)


def turn_tables():
    angles = np.arange(KG) * (2.0 * math.pi / KG)
    tables = []
    for values in (np.cos(angles), np.sin(angles)):
        values = values.astype(np.float32)
        high = values.astype(jnp.bfloat16).astype(np.float32)
        tables += [high, (values - high).astype(jnp.bfloat16).astype(np.float32)]
    return tables


def fetch(places, sems):
    copies = [
        pltpu.make_async_copy(start, end, sems.at[i]) for i, (start, end) in enumerate(places)
    ]
    for copy in copies:
        copy.start()
    return copies


def solve_kernel(grid_in, lattice_in, matrix_in, out, grid, lattice, matrix, wide, sems):
    kpoints, _, order, _ = matrix.shape
    own = order // 4
    chunk = out.shape[0] // own
    places = [(matrix_in.at[k, i], matrix.at[k, i]) for k in range(kpoints) for i in range(2)]
    copies = fetch(places + [(grid_in, grid), (lattice_in, lattice)], sems)
    row = lax.broadcasted_iota(jnp.int32, (own, order), 0)
    col = lax.broadcasted_iota(jnp.int32, (own, order), 1)
    pick = jnp.where(col == row * 4 + lax.axis_index("pair"), 1.0, 0.0).astype(BF16)
    first = []
    for k in range(kpoints):
        copies[2 * k].wait()
        copies[2 * k + 1].wait()
        first.append([dot(pick, matrix[k, part]) for part in range(2)])
    now = [list(pair) for pair in first]
    for step in range(ITERS - 1):
        for k in range(kpoints):
            re, im = now[k]
            re_high, im_high = re.astype(BF16), im.astype(BF16)
            parts = [re_high, im_high]
            if step > 0:
                parts.append((re - re_high.astype(F32)).astype(BF16))
                parts.append((im - im_high.astype(F32)).astype(BF16))
            left = jnp.concatenate(parts, axis=0)
            u = dot(left, matrix[k, 0])
            v = dot(left, matrix[k, 1])
            if step > 0:
                u = u[: 2 * own] + u[2 * own :]
                v = v[: 2 * own] + v[2 * own :]
            now[k] = [
                first[k][0] + u[:own] - v[own:],
                first[k][1] + v[:own] + u[own:],
            ]
    for k in range(kpoints):
        for part in range(2):
            for half in range(order // LANES):
                place = (k * 2 + part) * (order // LANES) + half
                wide[pl.ds(place, own, stride=chunk), :] = now[k][part][
                    :, half * LANES : (half + 1) * LANES
                ]
    copies[-2].wait()
    copies[-1].wait()
    vectors = lattice.shape[1]
    lane = lax.broadcasted_iota(jnp.int32, (8, LANES), 1)
    turn = jnp.zeros((8, LANES), jnp.int32)
    for r in range(vectors):
        for k in range(kpoints):
            m = (
                grid[k, 0] * lattice[0, r]
                + grid[k, 1] * lattice[1, r]
                + grid[k, 2] * lattice[2, r]
            ) & (KG - 1)
            here = ((lane // (4 * vectors)) == k) & ((lane & (vectors - 1)) == r)
            turn = jnp.where(here, m, turn)
    kind = (lane // vectors) & 3
    phase = jnp.zeros((8, LANES), F32)
    for which, table in enumerate(turn_tables()):
        for m in range(KG):
            phase = jnp.where((kind == which) & (turn == m), float(table[m]), phase)
    phase = jnp.broadcast_to(phase[:1], (own, LANES))
    wide[pl.ds(chunk - 2, own, stride=chunk), :] = phase
    wide[pl.ds(chunk - 1, own, stride=chunk), :] = jnp.zeros((own, LANES), F32)
    out[...] = wide[...].astype(BF16)


def phase_kernel(kpoints, vectors, rows, out, wide):
    chunk = 2 + 4 * kpoints
    sources = rows.shape[0] // chunk
    wide[...] = rows[...].astype(F32)
    info = wide[pl.ds(chunk - 2, sources, stride=chunk), :]
    info = jnp.transpose(info).astype(BF16)
    total = jnp.zeros((4 * vectors, 4 * LANES), F32)
    for k in range(kpoints):
        block = [wide[pl.ds(k * 4 + q, sources, stride=chunk), :] for q in range(4)]
        block = jnp.concatenate(block, axis=1).astype(BF16)
        total = total + dot(info[k * 4 * vectors : (k + 1) * 4 * vectors], block)
    cosine = total[:vectors] + total[vectors : 2 * vectors]
    sine = total[2 * vectors : 3 * vectors] + total[3 * vectors :]
    half = 2 * LANES
    re = cosine[:, :half] - sine[:, half:]
    im = cosine[:, half:] + sine[:, :half]
    both = jnp.concatenate([re, im], axis=1)
    out[...] = jnp.broadcast_to(both[None], out.shape)


def product_kernel(
    scale, parts, delta, route_in, species_in, count_in, host, out, wide, sums, *scratch
):
    vectors = parts.shape[1]
    kinds, _, order, _ = delta.shape
    route, species, count, sems = scratch
    slots, owners = route.shape
    copies = fetch([(route_in, route), (species_in, species), (count_in, count)], sems)
    pair, core = lax.axis_index("pair"), lax.axis_index("c")
    half = LANES // 2
    for q in range(4):
        sums[q * vectors : (q + 1) * vectors, :] = (parts[q] + parts[4 + q]) * scale
    odd = (pair & 1) == 1
    lane = lax.broadcasted_iota(jnp.int32, (1, LANES), 1)

    def window(re, im):
        re = jnp.where(odd, pltpu.roll(re, half, 1), re)
        im = jnp.where(odd, im, pltpu.roll(im, half, 1))
        return jnp.where(lane < half, re, im)

    own = pl.multiple_of(core * (2 * vectors), 2 * vectors)
    at = pl.multiple_of((pair // 2) * LANES, LANES)
    host[...] = window(
        sums[pl.ds(own, 2 * vectors), pl.ds(at, LANES)],
        sums[pl.ds(own, 2 * vectors), pl.ds(order + at, LANES)],
    )
    rows = 4 * vectors
    left = jnp.concatenate([sums[:, :order], sums[:, order:]], axis=0).astype(BF16)
    table = []
    for s in range(kinds):
        u = dot(left, delta[s, 0])
        v = dot(left, delta[s, 1])
        re = u[:rows] - v[rows:]
        im = v[:rows] + u[rows:]
        re = jnp.where(pair >= 2, re[:, LANES:], re[:, :LANES])
        im = jnp.where(pair >= 2, im[:, LANES:], im[:, :LANES])
        product = window(re, im)
        table.append(
            jnp.concatenate([product[q * vectors : (q + 1) * vectors] for q in range(4)], axis=1)
        )
    table = jnp.concatenate(table, axis=0).astype(BF16)
    for copy in copies:
        copy.wait()
    alive = lax.broadcasted_iota(jnp.int32, (slots, owners), 0) < count[...]
    combo = jnp.where(alive, species[...] * vectors + route[...], kinds * vectors)
    combo = jnp.transpose(combo.astype(F32)).astype(BF16)
    chips = owners // 2
    row = lax.broadcasted_iota(jnp.int32, (chips, owners), 0)
    col = lax.broadcasted_iota(jnp.int32, (chips, owners), 1)
    combo = dot(jnp.where(col == row * 2 + core, 1.0, 0.0).astype(BF16), combo)
    kind = lax.broadcasted_iota(jnp.int32, (chips, kinds * vectors), 1).astype(F32)
    chosen = [
        jnp.where(jnp.broadcast_to(combo[:, t : t + 1], kind.shape) == kind, 1.0, 0.0)
        for t in range(slots)
    ]
    chosen = jnp.concatenate(chosen, axis=0).astype(BF16)
    picked = dot(chosen, table)
    for t in range(slots):
        for q in range(4):
            wide[pl.ds(t * 4 + q, chips, stride=4 * slots), :] = picked[
                t * chips : (t + 1) * chips, q * LANES : (q + 1) * LANES
            ]
    out[...] = wide[...].astype(BF16)


def place_kernel(got, out, sems):
    copies = [
        pltpu.make_async_copy(got.at[:, t], out.at[t], sems.at[t]) for t in range(out.shape[0])
    ]
    for copy in copies:
        copy.start()
    for copy in copies:
        copy.wait()


VMEM = pl.BlockSpec(memory_space=pltpu.VMEM)
SMEM = pl.BlockSpec(memory_space=pltpu.SMEM)
HBM = pl.BlockSpec(memory_space=pltpu.HBM)


def in_hbm(x):
    return pltpu.with_memory_space_constraint(x, pltpu.HBM)


def params():
    return pltpu.CompilerParams(vmem_limit_bytes=32 * 1024 * 1024)


def per_device(kkr_matrix, kpoint_grid, lattice, delta_t, pair_count, pair_route, species):
    chips = lax.axis_size(CHIPS)
    cores = lax.axis_size(CORES)
    order = kkr_matrix.shape[2]
    kpoints = kkr_matrix.shape[0]
    vectors = lattice.shape[0]
    slots = pair_route.shape[1]
    scale = math.sqrt(order / (kpoints * chips * lax.axis_size("c")))
    chunk = 4 * kpoints + 2
    length = chips * chunk

    outgoing = pl.pallas_call(
        solve_kernel,
        out_shape=jax.ShapeDtypeStruct((length, LANES), BF16),
        in_specs=[HBM, HBM, HBM],
        out_specs=VMEM,
        scratch_shapes=[
            pltpu.SMEM((kpoints, 3), jnp.int32),
            pltpu.SMEM((3, vectors), jnp.int32),
            pltpu.VMEM(kkr_matrix.shape, BF16),
            pltpu.VMEM((length, LANES), F32),
            pltpu.SemaphoreType.DMA((2 * kpoints + 2,)),
        ],
        compiler_params=params(),
        name="solve",
    )(in_hbm(kpoint_grid), in_hbm(lattice.T), in_hbm(kkr_matrix))
    outgoing = outgoing.reshape(chips, chunk // 2, 2, LANES)
    arrived = lax.all_to_all(outgoing, CHIPS, split_axis=0, concat_axis=0, tiled=True)

    parts = pl.pallas_call(
        functools.partial(phase_kernel, kpoints, vectors),
        out_shape=jax.ShapeDtypeStruct((cores, vectors, 2 * order), F32),
        in_specs=[VMEM],
        out_specs=VMEM,
        scratch_shapes=[pltpu.VMEM((length, LANES), F32)],
        compiler_params=params(),
        name="phase_sum",
    )(arrived.reshape(length, LANES))
    parts = lax.all_to_all(parts, CORES, split_axis=0, concat_axis=0, tiled=True)

    host_rows, sent = pl.pallas_call(
        functools.partial(product_kernel, scale),
        out_shape=(
            jax.ShapeDtypeStruct((2 * vectors, LANES), F32),
            jax.ShapeDtypeStruct((chips * slots * 4, LANES), BF16),
        ),
        in_specs=[VMEM, VMEM, HBM, HBM, HBM],
        out_specs=(VMEM, VMEM),
        scratch_shapes=[
            pltpu.VMEM((chips * slots * 4, LANES), F32),
            pltpu.VMEM((4 * vectors, 2 * order), F32),
            pltpu.VMEM(pair_route.T.shape, jnp.int32),
            pltpu.VMEM(species.T.shape, jnp.int32),
            pltpu.VMEM((1,) + pair_count.shape, jnp.int32),
            pltpu.SemaphoreType.DMA((3,)),
        ],
        compiler_params=params(),
        name="product",
    )(parts, delta_t, in_hbm(pair_route.T), in_hbm(species.T), in_hbm(pair_count[None]))
    sent = sent.reshape(chips, slots * 4, LANES)
    got = lax.all_to_all(sent, CHIPS, split_axis=0, concat_axis=0, tiled=True)
    cluster = pl.pallas_call(
        place_kernel,
        out_shape=jax.ShapeDtypeStruct((slots, chips, 4, LANES), BF16),
        in_specs=[VMEM],
        out_specs=HBM,
        scratch_shapes=[pltpu.SemaphoreType.DMA((slots,))],
        compiler_params=params(),
        name="place",
    )(got.reshape(chips, slots, 4, LANES))
    return (host_rows, cluster.reshape(slots, order, LANES))


def solution(mesh):
    fine = Mesh(mesh.devices.reshape(8, 8, 2, 4), ("y", "z", "c", "pair"))
    ka = ("y", "z", "c")
    in_specs = (P(ka, None, None, None), P(ka, None), P(), P(), P(), P(), P())
    out_specs = (P(ka, "pair"), P(ka, None, "pair"))
    return jax.shard_map(
        per_device, mesh=fine, in_specs=in_specs, out_specs=out_specs, check_vma=False
    )
```

```python
import functools
import math

import jax
import jax.numpy as jnp
import numpy as np
from jax import lax
from jax.experimental import pallas as pl
from jax.experimental.pallas import tpu as pltpu
from jax.sharding import Mesh
from jax.sharding import PartitionSpec as P

ITERS = 6
KG = 16
LANES = 128
CHIPS = ("y", "z")
CORES = ("c", "pair")
F32 = jnp.float32
BF16 = jnp.bfloat16


def dot(a, b):
    return jnp.dot(a, b, preferred_element_type=F32)


def turn_tables():
    angles = np.arange(KG) * (2.0 * math.pi / KG)
    tables = []
    for values in (np.cos(angles), np.sin(angles)):
        values = values.astype(np.float32)
        high = values.astype(jnp.bfloat16).astype(np.float32)
        tables += [high, (values - high).astype(jnp.bfloat16).astype(np.float32)]
    return tables


def fetch(places, sems):
    copies = [
        pltpu.make_async_copy(start, end, sems.at[i]) for i, (start, end) in enumerate(places)
    ]
    for copy in copies:
        copy.start()
    return copies


def solve_kernel(
    kinds, grid_in, lattice_in, matrix_in, route_in, species_in, count_in, out, combo, *scratch
):
    grid, lattice, matrix, route, species, count, wide, sems = scratch
    kpoints, _, order, _ = matrix.shape
    own = order // 4
    chunk = out.shape[0] // own
    places = [(matrix_in.at[k, i], matrix.at[k, i]) for k in range(kpoints) for i in range(2)]
    places = [(grid_in, grid), (lattice_in, lattice)] + places
    places += [(route_in, route), (species_in, species), (count_in, count)]
    copies = fetch(places, sems)
    small, large, late = copies[:2], copies[2:-3], copies[-3:]
    for copy in small:
        copy.wait()
    vectors = lattice.shape[1]
    lane = lax.broadcasted_iota(jnp.int32, (8, LANES), 1)
    turn = jnp.zeros((8, LANES), jnp.int32)
    for r in range(vectors):
        for k in range(kpoints):
            m = (
                grid[k, 0] * lattice[0, r]
                + grid[k, 1] * lattice[1, r]
                + grid[k, 2] * lattice[2, r]
            ) & (KG - 1)
            here = ((lane // (4 * vectors)) == k) & ((lane & (vectors - 1)) == r)
            turn = jnp.where(here, m, turn)
    kind = (lane // vectors) & 3
    phase = jnp.zeros((8, LANES), F32)
    for which, table in enumerate(turn_tables()):
        for m in range(KG):
            phase = jnp.where((kind == which) & (turn == m), float(table[m]), phase)
    phase = jnp.broadcast_to(phase[:1], (own, LANES))
    wide[pl.ds(chunk - 2, own, stride=chunk), :] = phase
    wide[pl.ds(chunk - 1, own, stride=chunk), :] = jnp.zeros((own, LANES), F32)
    row = lax.broadcasted_iota(jnp.int32, (own, order), 0)
    col = lax.broadcasted_iota(jnp.int32, (own, order), 1)
    pick = jnp.where(col == row * 4 + lax.axis_index("pair"), 1.0, 0.0).astype(BF16)
    first = []
    for k in range(kpoints):
        large[2 * k].wait()
        large[2 * k + 1].wait()
        first.append([dot(pick, matrix[k, part]) for part in range(2)])
    now = [list(pair) for pair in first]
    for step in range(ITERS - 1):
        for k in range(kpoints):
            re, im = now[k]
            re_high, im_high = re.astype(BF16), im.astype(BF16)
            parts = [re_high, im_high]
            if step > 0:
                parts.append((re - re_high.astype(F32)).astype(BF16))
                parts.append((im - im_high.astype(F32)).astype(BF16))
            left = jnp.concatenate(parts, axis=0)
            u = dot(left, matrix[k, 0])
            v = dot(left, matrix[k, 1])
            if step > 0:
                u = u[: 2 * own] + u[2 * own :]
                v = v[: 2 * own] + v[2 * own :]
            now[k] = [
                first[k][0] + u[:own] - v[own:],
                first[k][1] + v[:own] + u[own:],
            ]
    for k in range(kpoints):
        for part in range(2):
            for half in range(order // LANES):
                place = (k * 2 + part) * (order // LANES) + half
                wide[pl.ds(place, own, stride=chunk), :] = now[k][part][
                    :, half * LANES : (half + 1) * LANES
                ]
    for copy in late:
        copy.wait()
    alive = lax.broadcasted_iota(jnp.int32, combo.shape, 0) < count[...]
    combo[...] = jnp.where(alive, species[...] * vectors + route[...], kinds * vectors)
    out[...] = wide[...].astype(BF16)


def phase_kernel(kpoints, vectors, rows, out, wide):
    chunk = 2 + 4 * kpoints
    sources = rows.shape[0] // chunk
    wide[...] = rows[...].astype(F32)
    info = wide[pl.ds(chunk - 2, sources, stride=chunk), :]
    info = jnp.transpose(info).astype(BF16)
    total = jnp.zeros((4 * vectors, 4 * LANES), F32)
    for k in range(kpoints):
        block = [wide[pl.ds(k * 4 + q, sources, stride=chunk), :] for q in range(4)]
        block = jnp.concatenate(block, axis=1).astype(BF16)
        total = total + dot(info[k * 4 * vectors : (k + 1) * 4 * vectors], block)
    cosine = total[:vectors] + total[vectors : 2 * vectors]
    sine = total[2 * vectors : 3 * vectors] + total[3 * vectors :]
    half = 2 * LANES
    re = cosine[:, :half] - sine[:, half:]
    im = cosine[:, half:] + sine[:, :half]
    both = jnp.concatenate([re, im], axis=1)
    out[...] = jnp.broadcast_to(both[None], out.shape)


def product_kernel(scale, parts, delta, combo, host, out, wide, sums):
    vectors = parts.shape[1]
    kinds, _, order, _ = delta.shape
    slots, owners = combo.shape
    pair, core = lax.axis_index("pair"), lax.axis_index("c")
    half = LANES // 2
    for q in range(4):
        sums[q * vectors : (q + 1) * vectors, :] = (parts[q] + parts[4 + q]) * scale
    odd = (pair & 1) == 1
    lane = lax.broadcasted_iota(jnp.int32, (1, LANES), 1)

    def window(re, im):
        re = jnp.where(odd, pltpu.roll(re, half, 1), re)
        im = jnp.where(odd, im, pltpu.roll(im, half, 1))
        return jnp.where(lane < half, re, im)

    own = pl.multiple_of(core * (2 * vectors), 2 * vectors)
    at = pl.multiple_of((pair // 2) * LANES, LANES)
    host[...] = window(
        sums[pl.ds(own, 2 * vectors), pl.ds(at, LANES)],
        sums[pl.ds(own, 2 * vectors), pl.ds(order + at, LANES)],
    )
    rows = 4 * vectors
    left = jnp.concatenate([sums[:, :order], sums[:, order:]], axis=0).astype(BF16)
    table = []
    for s in range(kinds):
        u = dot(left, delta[s, 0])
        v = dot(left, delta[s, 1])
        re = u[:rows] - v[rows:]
        im = v[:rows] + u[rows:]
        re = jnp.where(pair >= 2, re[:, LANES:], re[:, :LANES])
        im = jnp.where(pair >= 2, im[:, LANES:], im[:, :LANES])
        product = window(re, im)
        table.append(
            jnp.concatenate([product[q * vectors : (q + 1) * vectors] for q in range(4)], axis=1)
        )
    table = jnp.concatenate(table, axis=0).astype(BF16)
    combo = jnp.transpose(combo[...].astype(F32)).astype(BF16)
    chips = owners // 2
    row = lax.broadcasted_iota(jnp.int32, (chips, owners), 0)
    col = lax.broadcasted_iota(jnp.int32, (chips, owners), 1)
    combo = dot(jnp.where(col == row * 2 + core, 1.0, 0.0).astype(BF16), combo)
    kind = lax.broadcasted_iota(jnp.int32, (chips, kinds * vectors), 1).astype(F32)
    chosen = [
        jnp.where(jnp.broadcast_to(combo[:, t : t + 1], kind.shape) == kind, 1.0, 0.0)
        for t in range(slots)
    ]
    chosen = jnp.concatenate(chosen, axis=0).astype(BF16)
    picked = dot(chosen, table)
    for t in range(slots):
        for q in range(4):
            wide[pl.ds(t * 4 + q, chips, stride=4 * slots), :] = picked[
                t * chips : (t + 1) * chips, q * LANES : (q + 1) * LANES
            ]
    out[...] = wide[...].astype(BF16)


def place_kernel(got, out, sems):
    slots, chips = out.shape[:2]
    cut = sems.shape[0] // slots
    size = chips // cut
    places = [
        (got.at[i * size : (i + 1) * size, t], out.at[t, i * size : (i + 1) * size])
        for t in range(slots)
        for i in range(cut)
    ]
    for copy in fetch(places, sems):
        copy.wait()


VMEM = pl.BlockSpec(memory_space=pltpu.VMEM)
SMEM = pl.BlockSpec(memory_space=pltpu.SMEM)
HBM = pl.BlockSpec(memory_space=pltpu.HBM)


def in_hbm(x):
    return pltpu.with_memory_space_constraint(x, pltpu.HBM)


def params():
    return pltpu.CompilerParams(vmem_limit_bytes=32 * 1024 * 1024)


def per_device(kkr_matrix, kpoint_grid, lattice, delta_t, pair_count, pair_route, species):
    chips = lax.axis_size(CHIPS)
    cores = lax.axis_size(CORES)
    order = kkr_matrix.shape[2]
    kpoints = kkr_matrix.shape[0]
    vectors = lattice.shape[0]
    slots = pair_route.shape[1]
    kinds = delta_t.shape[0]
    scale = math.sqrt(order / (kpoints * chips * lax.axis_size("c")))
    chunk = 4 * kpoints + 2
    length = chips * chunk

    route, kind, count = pair_route.T, species.T, pair_count[None]
    outgoing, combo = pl.pallas_call(
        functools.partial(solve_kernel, kinds),
        out_shape=(
            jax.ShapeDtypeStruct((length, LANES), BF16),
            jax.ShapeDtypeStruct(route.shape, jnp.int32),
        ),
        in_specs=[HBM] * 6,
        out_specs=(VMEM, VMEM),
        scratch_shapes=[
            pltpu.SMEM((kpoints, 3), jnp.int32),
            pltpu.SMEM((3, vectors), jnp.int32),
            pltpu.VMEM(kkr_matrix.shape, BF16),
            pltpu.VMEM(route.shape, jnp.int32),
            pltpu.VMEM(kind.shape, jnp.int32),
            pltpu.VMEM(count.shape, jnp.int32),
            pltpu.VMEM((length, LANES), F32),
            pltpu.SemaphoreType.DMA((2 * kpoints + 5,)),
        ],
        compiler_params=params(),
        name="solve",
    )(*map(in_hbm, (kpoint_grid, lattice.T, kkr_matrix, route, kind, count)))
    outgoing = outgoing.reshape(chips, chunk // 2, 2, LANES)
    arrived = lax.all_to_all(outgoing, CHIPS, split_axis=0, concat_axis=0, tiled=True)

    parts = pl.pallas_call(
        functools.partial(phase_kernel, kpoints, vectors),
        out_shape=jax.ShapeDtypeStruct((cores, vectors, 2 * order), F32),
        in_specs=[VMEM],
        out_specs=VMEM,
        scratch_shapes=[pltpu.VMEM((length, LANES), F32)],
        compiler_params=params(),
        name="phase_sum",
    )(arrived.reshape(length, LANES))
    parts = lax.all_to_all(parts, CORES, split_axis=0, concat_axis=0, tiled=True)

    host_rows, sent = pl.pallas_call(
        functools.partial(product_kernel, scale),
        out_shape=(
            jax.ShapeDtypeStruct((2 * vectors, LANES), F32),
            jax.ShapeDtypeStruct((chips * slots * 4, LANES), BF16),
        ),
        in_specs=[VMEM, VMEM, VMEM],
        out_specs=(VMEM, VMEM),
        scratch_shapes=[
            pltpu.VMEM((chips * slots * 4, LANES), F32),
            pltpu.VMEM((4 * vectors, 2 * order), F32),
        ],
        compiler_params=params(),
        name="product",
    )(parts, delta_t, combo)
    sent = sent.reshape(chips, slots * 4, LANES)
    got = lax.all_to_all(sent, CHIPS, split_axis=0, concat_axis=0, tiled=True)
    cluster = pl.pallas_call(
        place_kernel,
        out_shape=jax.ShapeDtypeStruct((slots, chips, 4, LANES), BF16),
        in_specs=[VMEM],
        out_specs=HBM,
        scratch_shapes=[pltpu.SemaphoreType.DMA((4 * slots,))],
        compiler_params=params(),
        name="place",
    )(got.reshape(chips, slots, 4, LANES))
    return (host_rows, cluster.reshape(slots, order, LANES))


def solution(mesh):
    fine = Mesh(mesh.devices.reshape(8, 8, 2, 4), ("y", "z", "c", "pair"))
    ka = ("y", "z", "c")
    in_specs = (P(ka, None, None, None), P(ka, None), P(), P(), P(), P(), P())
    out_specs = (P(ka, "pair"), P(ka, None, "pair"))
    return jax.shard_map(
        per_device, mesh=fine, in_specs=in_specs, out_specs=out_specs, check_vma=False
    )
```

```python
import functools
import math

import jax
import jax.numpy as jnp
import numpy as np
from jax import lax
from jax.experimental import pallas as pl
from jax.experimental.pallas import tpu as pltpu
from jax.sharding import Mesh
from jax.sharding import PartitionSpec as P

ITERS = 6
KG = 16
LANES = 128
CHIPS = ("y", "z")
CORES = ("c", "pair")
F32 = jnp.float32
BF16 = jnp.bfloat16


def dot(a, b):
    return jnp.dot(a, b, preferred_element_type=F32)


def turn_tables():
    angles = np.arange(KG) * (2.0 * math.pi / KG)
    tables = []
    for values in (np.cos(angles), np.sin(angles)):
        values = values.astype(np.float32)
        high = values.astype(jnp.bfloat16).astype(np.float32)
        tables += [high, (values - high).astype(jnp.bfloat16).astype(np.float32)]
    return tables


def fetch(places, sems):
    copies = [
        pltpu.make_async_copy(start, end, sems.at[i]) for i, (start, end) in enumerate(places)
    ]
    for copy in copies:
        copy.start()
    return copies


def solve_kernel(
    kinds, grid_in, lattice_in, matrix_in, route_in, species_in, count_in, out, combo, *scratch
):
    grid, lattice, matrix, route, species, count, wide, sems = scratch
    kpoints, _, order, _ = matrix.shape
    own = order // 4
    chunk = out.shape[0] // own
    places = [(matrix_in.at[k, i], matrix.at[k, i]) for k in range(kpoints) for i in range(2)]
    places = [(grid_in, grid), (lattice_in, lattice)] + places
    places += [(route_in, route), (species_in, species), (count_in, count)]
    copies = fetch(places, sems)
    small, large, late = copies[:2], copies[2:-3], copies[-3:]
    for copy in small:
        copy.wait()
    vectors = lattice.shape[1]
    lane = lax.broadcasted_iota(jnp.int32, (8, LANES), 1)
    turn = jnp.zeros((8, LANES), jnp.int32)
    for r in range(vectors):
        for k in range(kpoints):
            m = (
                grid[k, 0] * lattice[0, r]
                + grid[k, 1] * lattice[1, r]
                + grid[k, 2] * lattice[2, r]
            ) & (KG - 1)
            here = ((lane // (4 * vectors)) == k) & ((lane & (vectors - 1)) == r)
            turn = jnp.where(here, m, turn)
    kind = (lane // vectors) & 3
    phase = jnp.zeros((8, LANES), F32)
    for which, table in enumerate(turn_tables()):
        for m in range(KG):
            phase = jnp.where((kind == which) & (turn == m), float(table[m]), phase)
    phase = jnp.broadcast_to(phase[:1], (own, LANES))
    wide[pl.ds(chunk - 2, own, stride=chunk), :] = phase
    wide[pl.ds(chunk - 1, own, stride=chunk), :] = jnp.zeros((own, LANES), F32)
    row = lax.broadcasted_iota(jnp.int32, (own, order), 0)
    col = lax.broadcasted_iota(jnp.int32, (own, order), 1)
    pick = jnp.where(col == row * 4 + lax.axis_index("pair"), 1.0, 0.0).astype(BF16)
    first = []
    for k in range(kpoints):
        large[2 * k].wait()
        large[2 * k + 1].wait()
        first.append([dot(pick, matrix[k, part]) for part in range(2)])
    now = [list(pair) for pair in first]
    for step in range(ITERS - 1):
        for k in range(kpoints):
            re, im = now[k]
            re_high, im_high = re.astype(BF16), im.astype(BF16)
            parts = [re_high, im_high]
            if step > 0:
                parts.append((re - re_high.astype(F32)).astype(BF16))
                parts.append((im - im_high.astype(F32)).astype(BF16))
            left = jnp.concatenate(parts, axis=0)
            u = dot(left, matrix[k, 0])
            v = dot(left, matrix[k, 1])
            if step > 0:
                u = u[: 2 * own] + u[2 * own :]
                v = v[: 2 * own] + v[2 * own :]
            now[k] = [
                first[k][0] + u[:own] - v[own:],
                first[k][1] + v[:own] + u[own:],
            ]
    for k in range(kpoints):
        for part in range(2):
            for half in range(order // LANES):
                place = (k * 2 + part) * (order // LANES) + half
                wide[pl.ds(place, own, stride=chunk), :] = now[k][part][
                    :, half * LANES : (half + 1) * LANES
                ]
    for copy in late:
        copy.wait()
    alive = lax.broadcasted_iota(jnp.int32, combo.shape, 0) < count[...]
    combo[...] = jnp.where(alive, species[...] * vectors + route[...], kinds * vectors)
    out[...] = wide[...].astype(BF16)


def phase_kernel(kpoints, vectors, rows, out, wide):
    chunk = 2 + 4 * kpoints
    sources = rows.shape[0] // chunk
    wide[...] = rows[...].astype(F32)
    info = wide[pl.ds(chunk - 2, sources, stride=chunk), :]
    info = jnp.transpose(info).astype(BF16)
    total = jnp.zeros((4 * vectors, 4 * LANES), F32)
    for k in range(kpoints):
        block = [wide[pl.ds(k * 4 + q, sources, stride=chunk), :] for q in range(4)]
        block = jnp.concatenate(block, axis=1).astype(BF16)
        total = total + dot(info[k * 4 * vectors : (k + 1) * 4 * vectors], block)
    cosine = total[:vectors] + total[vectors : 2 * vectors]
    sine = total[2 * vectors : 3 * vectors] + total[3 * vectors :]
    half = 2 * LANES
    re = cosine[:, :half] - sine[:, half:]
    im = cosine[:, half:] + sine[:, :half]
    both = jnp.concatenate([re, im], axis=1).astype(BF16)
    out[...] = jnp.broadcast_to(both[None], out.shape)


def product_kernel(scale, parts, delta, combo, host, out, wide, sums):
    vectors = parts.shape[1]
    kinds, _, order, _ = delta.shape
    slots, owners = combo.shape
    pair, core = lax.axis_index("pair"), lax.axis_index("c")
    half = LANES // 2
    for q in range(4):
        sums[q * vectors : (q + 1) * vectors, :] = (
            parts[q].astype(F32) + parts[4 + q].astype(F32)
        ) * scale
    odd = (pair & 1) == 1
    lane = lax.broadcasted_iota(jnp.int32, (1, LANES), 1)

    def window(re, im):
        re = jnp.where(odd, pltpu.roll(re, half, 1), re)
        im = jnp.where(odd, im, pltpu.roll(im, half, 1))
        return jnp.where(lane < half, re, im)

    own = pl.multiple_of(core * (2 * vectors), 2 * vectors)
    at = pl.multiple_of((pair // 2) * LANES, LANES)
    host[...] = window(
        sums[pl.ds(own, 2 * vectors), pl.ds(at, LANES)],
        sums[pl.ds(own, 2 * vectors), pl.ds(order + at, LANES)],
    )
    rows = 4 * vectors
    left = jnp.concatenate([sums[:, :order], sums[:, order:]], axis=0).astype(BF16)
    table = []
    for s in range(kinds):
        u = dot(left, delta[s, 0])
        v = dot(left, delta[s, 1])
        re = u[:rows] - v[rows:]
        im = v[:rows] + u[rows:]
        re = jnp.where(pair >= 2, re[:, LANES:], re[:, :LANES])
        im = jnp.where(pair >= 2, im[:, LANES:], im[:, :LANES])
        product = window(re, im)
        table.append(
            jnp.concatenate([product[q * vectors : (q + 1) * vectors] for q in range(4)], axis=1)
        )
    table = jnp.concatenate(table, axis=0).astype(BF16)
    combo = jnp.transpose(combo[...].astype(F32)).astype(BF16)
    chips = owners // 2
    row = lax.broadcasted_iota(jnp.int32, (chips, owners), 0)
    col = lax.broadcasted_iota(jnp.int32, (chips, owners), 1)
    combo = dot(jnp.where(col == row * 2 + core, 1.0, 0.0).astype(BF16), combo)
    kind = lax.broadcasted_iota(jnp.int32, (chips, kinds * vectors), 1).astype(F32)
    chosen = [
        jnp.where(jnp.broadcast_to(combo[:, t : t + 1], kind.shape) == kind, 1.0, 0.0)
        for t in range(slots)
    ]
    chosen = jnp.concatenate(chosen, axis=0).astype(BF16)
    picked = dot(chosen, table)
    for t in range(slots):
        for q in range(4):
            wide[pl.ds(t * 4 + q, chips, stride=4 * slots), :] = picked[
                t * chips : (t + 1) * chips, q * LANES : (q + 1) * LANES
            ]
    out[...] = wide[...].astype(BF16)


def place_kernel(got, out, sems):
    places = [(got.at[:, t], out.at[t]) for t in range(out.shape[0])]
    for copy in fetch(places, sems):
        copy.wait()


VMEM = pl.BlockSpec(memory_space=pltpu.VMEM)
SMEM = pl.BlockSpec(memory_space=pltpu.SMEM)
HBM = pl.BlockSpec(memory_space=pltpu.HBM)


def in_hbm(x):
    return pltpu.with_memory_space_constraint(x, pltpu.HBM)


def params():
    return pltpu.CompilerParams(vmem_limit_bytes=32 * 1024 * 1024)


def per_device(kkr_matrix, kpoint_grid, lattice, delta_t, pair_count, pair_route, species):
    chips = lax.axis_size(CHIPS)
    cores = lax.axis_size(CORES)
    order = kkr_matrix.shape[2]
    kpoints = kkr_matrix.shape[0]
    vectors = lattice.shape[0]
    slots = pair_route.shape[1]
    kinds = delta_t.shape[0]
    scale = math.sqrt(order / (kpoints * chips * lax.axis_size("c")))
    chunk = 4 * kpoints + 2
    length = chips * chunk

    route, kind, count = pair_route.T, species.T, pair_count[None]
    outgoing, combo = pl.pallas_call(
        functools.partial(solve_kernel, kinds),
        out_shape=(
            jax.ShapeDtypeStruct((length, LANES), BF16),
            jax.ShapeDtypeStruct(route.shape, jnp.int32),
        ),
        in_specs=[HBM] * 6,
        out_specs=(VMEM, VMEM),
        scratch_shapes=[
            pltpu.SMEM((kpoints, 3), jnp.int32),
            pltpu.SMEM((3, vectors), jnp.int32),
            pltpu.VMEM(kkr_matrix.shape, BF16),
            pltpu.VMEM(route.shape, jnp.int32),
            pltpu.VMEM(kind.shape, jnp.int32),
            pltpu.VMEM(count.shape, jnp.int32),
            pltpu.VMEM((length, LANES), F32),
            pltpu.SemaphoreType.DMA((2 * kpoints + 5,)),
        ],
        compiler_params=params(),
        name="solve",
    )(*map(in_hbm, (kpoint_grid, lattice.T, kkr_matrix, route, kind, count)))
    outgoing = outgoing.reshape(chips, chunk // 2, 2, LANES)
    arrived = lax.all_to_all(outgoing, CHIPS, split_axis=0, concat_axis=0, tiled=True)

    parts = pl.pallas_call(
        functools.partial(phase_kernel, kpoints, vectors),
        out_shape=jax.ShapeDtypeStruct((cores, vectors, 2 * order), BF16),
        in_specs=[VMEM],
        out_specs=VMEM,
        scratch_shapes=[pltpu.VMEM((length, LANES), F32)],
        compiler_params=params(),
        name="phase_sum",
    )(arrived.reshape(length, LANES))
    parts = lax.all_to_all(parts, CORES, split_axis=0, concat_axis=0, tiled=True)

    host_rows, sent = pl.pallas_call(
        functools.partial(product_kernel, scale),
        out_shape=(
            jax.ShapeDtypeStruct((2 * vectors, LANES), F32),
            jax.ShapeDtypeStruct((chips * slots * 4, LANES), BF16),
        ),
        in_specs=[VMEM, VMEM, VMEM],
        out_specs=(VMEM, VMEM),
        scratch_shapes=[
            pltpu.VMEM((chips * slots * 4, LANES), F32),
            pltpu.VMEM((4 * vectors, 2 * order), F32),
        ],
        compiler_params=params(),
        name="product",
    )(parts, delta_t, combo)
    sent = sent.reshape(chips, slots * 4, LANES)
    got = lax.all_to_all(sent, CHIPS, split_axis=0, concat_axis=0, tiled=True)
    cluster = pl.pallas_call(
        place_kernel,
        out_shape=jax.ShapeDtypeStruct((slots, chips, 4, LANES), BF16),
        in_specs=[VMEM],
        out_specs=HBM,
        scratch_shapes=[pltpu.SemaphoreType.DMA((slots,))],
        compiler_params=params(),
        name="place",
    )(got.reshape(chips, slots, 4, LANES))
    return (host_rows, cluster.reshape(slots, order, LANES))


def solution(mesh):
    fine = Mesh(mesh.devices.reshape(8, 8, 2, 4), ("y", "z", "c", "pair"))
    ka = ("y", "z", "c")
    in_specs = (P(ka, None, None, None), P(ka, None), P(), P(), P(), P(), P())
    out_specs = (P(ka, "pair"), P(ka, None, "pair"))
    return jax.shard_map(
        per_device, mesh=fine, in_specs=in_specs, out_specs=out_specs, check_vma=False
    )
```

```python
import functools
import math

import jax
import jax.numpy as jnp
import numpy as np
from jax import lax
from jax.experimental import pallas as pl
from jax.experimental.pallas import tpu as pltpu
from jax.sharding import Mesh
from jax.sharding import PartitionSpec as P

ITERS = 6
KG = 16
LANES = 128
CHIPS = ("y", "z")
CORES = ("c", "pair")
F32 = jnp.float32
BF16 = jnp.bfloat16


def dot(a, b):
    return jnp.dot(a, b, preferred_element_type=F32)


def turn_tables():
    angles = np.arange(KG) * (2.0 * math.pi / KG)
    tables = []
    for values in (np.cos(angles), np.sin(angles)):
        values = values.astype(np.float32)
        high = values.astype(jnp.bfloat16).astype(np.float32)
        tables += [high, (values - high).astype(jnp.bfloat16).astype(np.float32)]
    return tables


def fetch(places, sems):
    copies = [
        pltpu.make_async_copy(start, end, sems.at[i]) for i, (start, end) in enumerate(places)
    ]
    for copy in copies:
        copy.start()
    return copies


def solve_kernel(
    kinds, grid_in, lattice_in, matrix_in, route_in, species_in, count_in, out, chosen, *scratch
):
    grid, lattice, matrix, route, species, count, wide, sems = scratch
    kpoints, _, order, _ = matrix.shape
    own = order // 4
    chunk = out.shape[0] // own
    places = [(matrix_in.at[k, i], matrix.at[k, i]) for k in range(kpoints) for i in range(2)]
    small = [(grid_in, grid), (lattice_in, lattice), (route_in, route), (species_in, species)]
    small += [(count_in, count)]
    copies = fetch(small + places, sems)
    small, large = copies[: len(small)], copies[len(small) :]
    for copy in small:
        copy.wait()
    vectors = lattice.shape[1]
    lane = lax.broadcasted_iota(jnp.int32, (8, LANES), 1)
    turn = jnp.zeros((8, LANES), jnp.int32)
    for r in range(vectors):
        for k in range(kpoints):
            m = (
                grid[k, 0] * lattice[0, r]
                + grid[k, 1] * lattice[1, r]
                + grid[k, 2] * lattice[2, r]
            ) & (KG - 1)
            here = ((lane // (4 * vectors)) == k) & ((lane & (vectors - 1)) == r)
            turn = jnp.where(here, m, turn)
    kind = (lane // vectors) & 3
    phase = jnp.zeros((8, LANES), F32)
    for which, table in enumerate(turn_tables()):
        for m in range(KG):
            phase = jnp.where((kind == which) & (turn == m), float(table[m]), phase)
    phase = jnp.broadcast_to(phase[:1], (own, LANES))
    wide[pl.ds(chunk - 2, own, stride=chunk), :] = phase
    wide[pl.ds(chunk - 1, own, stride=chunk), :] = jnp.zeros((own, LANES), F32)
    slots, owners = route.shape
    chips = owners // 2
    alive = lax.broadcasted_iota(jnp.int32, (slots, owners), 0) < count[...]
    combo = jnp.where(alive, species[...] * vectors + route[...], kinds * vectors)
    combo = jnp.transpose(combo.astype(F32)).astype(BF16)
    row = lax.broadcasted_iota(jnp.int32, (chips, owners), 0)
    col = lax.broadcasted_iota(jnp.int32, (chips, owners), 1)
    mine = jnp.where(col == row * 2 + lax.axis_index("c"), 1.0, 0.0).astype(BF16)
    combo = dot(mine, combo)
    which = lax.broadcasted_iota(jnp.int32, (chips, kinds * vectors), 1).astype(F32)
    for t in range(slots):
        hit = jnp.broadcast_to(combo[:, t : t + 1], which.shape) == which
        chosen[t * chips : (t + 1) * chips, :] = jnp.where(hit, 1.0, 0.0).astype(BF16)
    row = lax.broadcasted_iota(jnp.int32, (own, order), 0)
    col = lax.broadcasted_iota(jnp.int32, (own, order), 1)
    pick = jnp.where(col == row * 4 + lax.axis_index("pair"), 1.0, 0.0).astype(BF16)
    first = []
    for k in range(kpoints):
        large[2 * k].wait()
        large[2 * k + 1].wait()
        first.append([dot(pick, matrix[k, part]) for part in range(2)])
    now = [list(pair) for pair in first]
    for step in range(ITERS - 1):
        for k in range(kpoints):
            re, im = now[k]
            re_high, im_high = re.astype(BF16), im.astype(BF16)
            parts = [re_high, im_high]
            if step > 0:
                parts.append((re - re_high.astype(F32)).astype(BF16))
                parts.append((im - im_high.astype(F32)).astype(BF16))
            left = jnp.concatenate(parts, axis=0)
            u = dot(left, matrix[k, 0])
            v = dot(left, matrix[k, 1])
            if step > 0:
                u = u[: 2 * own] + u[2 * own :]
                v = v[: 2 * own] + v[2 * own :]
            now[k] = [
                first[k][0] + u[:own] - v[own:],
                first[k][1] + v[:own] + u[own:],
            ]
    for k in range(kpoints):
        for part in range(2):
            for half in range(order // LANES):
                place = (k * 2 + part) * (order // LANES) + half
                wide[pl.ds(place, own, stride=chunk), :] = now[k][part][
                    :, half * LANES : (half + 1) * LANES
                ]
    out[...] = wide[...].astype(BF16)


def phase_kernel(kpoints, vectors, rows, out, wide):
    chunk = 2 + 4 * kpoints
    sources = rows.shape[0] // chunk
    wide[...] = rows[...].astype(F32)
    info = wide[pl.ds(chunk - 2, sources, stride=chunk), :]
    info = jnp.transpose(info).astype(BF16)
    total = jnp.zeros((4 * vectors, 4 * LANES), F32)
    for k in range(kpoints):
        block = [wide[pl.ds(k * 4 + q, sources, stride=chunk), :] for q in range(4)]
        block = jnp.concatenate(block, axis=1).astype(BF16)
        total = total + dot(info[k * 4 * vectors : (k + 1) * 4 * vectors], block)
    cosine = total[:vectors] + total[vectors : 2 * vectors]
    sine = total[2 * vectors : 3 * vectors] + total[3 * vectors :]
    half = 2 * LANES
    re = cosine[:, :half] - sine[:, half:]
    im = cosine[:, half:] + sine[:, :half]
    both = jnp.concatenate([re, im], axis=1)
    out[...] = jnp.broadcast_to(both[None], out.shape)


def product_kernel(scale, slots, parts, delta, chosen, host, out, wide, sums):
    vectors = parts.shape[1]
    kinds, _, order, _ = delta.shape
    pair, core = lax.axis_index("pair"), lax.axis_index("c")
    half = LANES // 2
    for q in range(4):
        sums[q * vectors : (q + 1) * vectors, :] = (parts[q] + parts[4 + q]) * scale
    odd = (pair & 1) == 1
    lane = lax.broadcasted_iota(jnp.int32, (1, LANES), 1)

    def window(re, im):
        re = jnp.where(odd, pltpu.roll(re, half, 1), re)
        im = jnp.where(odd, im, pltpu.roll(im, half, 1))
        return jnp.where(lane < half, re, im)

    own = pl.multiple_of(core * (2 * vectors), 2 * vectors)
    at = pl.multiple_of((pair // 2) * LANES, LANES)
    host[...] = window(
        sums[pl.ds(own, 2 * vectors), pl.ds(at, LANES)],
        sums[pl.ds(own, 2 * vectors), pl.ds(order + at, LANES)],
    )
    rows = 4 * vectors
    left = jnp.concatenate([sums[:, :order], sums[:, order:]], axis=0).astype(BF16)
    table = []
    for s in range(kinds):
        u = dot(left, delta[s, 0])
        v = dot(left, delta[s, 1])
        re = u[:rows] - v[rows:]
        im = v[:rows] + u[rows:]
        re = jnp.where(pair >= 2, re[:, LANES:], re[:, :LANES])
        im = jnp.where(pair >= 2, im[:, LANES:], im[:, :LANES])
        product = window(re, im)
        table.append(
            jnp.concatenate([product[q * vectors : (q + 1) * vectors] for q in range(4)], axis=1)
        )
    table = jnp.concatenate(table, axis=0).astype(BF16)
    chips = chosen.shape[0] // slots
    picked = dot(chosen[...], table)
    for t in range(slots):
        for q in range(4):
            wide[pl.ds(t * 4 + q, chips, stride=4 * slots), :] = picked[
                t * chips : (t + 1) * chips, q * LANES : (q + 1) * LANES
            ]
    out[...] = wide[...].astype(BF16)


def place_kernel(got, out, sems):
    places = [(got.at[:, t], out.at[t]) for t in range(out.shape[0])]
    for copy in fetch(places, sems):
        copy.wait()


VMEM = pl.BlockSpec(memory_space=pltpu.VMEM)
SMEM = pl.BlockSpec(memory_space=pltpu.SMEM)
HBM = pl.BlockSpec(memory_space=pltpu.HBM)


def in_hbm(x):
    return pltpu.with_memory_space_constraint(x, pltpu.HBM)


def params():
    return pltpu.CompilerParams(vmem_limit_bytes=32 * 1024 * 1024)


def per_device(kkr_matrix, kpoint_grid, lattice, delta_t, pair_count, pair_route, species):
    chips = lax.axis_size(CHIPS)
    cores = lax.axis_size(CORES)
    order = kkr_matrix.shape[2]
    kpoints = kkr_matrix.shape[0]
    vectors = lattice.shape[0]
    slots = pair_route.shape[1]
    kinds = delta_t.shape[0]
    scale = math.sqrt(order / (kpoints * chips * lax.axis_size("c")))
    chunk = 4 * kpoints + 2
    length = chips * chunk

    route, kind, count = pair_route.T, species.T, pair_count[None]
    outgoing, chosen = pl.pallas_call(
        functools.partial(solve_kernel, kinds),
        out_shape=(
            jax.ShapeDtypeStruct((length, LANES), BF16),
            jax.ShapeDtypeStruct((chips * slots, kinds * vectors), BF16),
        ),
        in_specs=[HBM] * 6,
        out_specs=(VMEM, VMEM),
        scratch_shapes=[
            pltpu.SMEM((kpoints, 3), jnp.int32),
            pltpu.SMEM((3, vectors), jnp.int32),
            pltpu.VMEM(kkr_matrix.shape, BF16),
            pltpu.VMEM(route.shape, jnp.int32),
            pltpu.VMEM(kind.shape, jnp.int32),
            pltpu.VMEM(count.shape, jnp.int32),
            pltpu.VMEM((length, LANES), F32),
            pltpu.SemaphoreType.DMA((2 * kpoints + 5,)),
        ],
        compiler_params=params(),
        name="solve",
    )(*map(in_hbm, (kpoint_grid, lattice.T, kkr_matrix, route, kind, count)))
    outgoing = outgoing.reshape(chips, chunk // 2, 2, LANES)
    arrived = lax.all_to_all(outgoing, CHIPS, split_axis=0, concat_axis=0, tiled=True)

    parts = pl.pallas_call(
        functools.partial(phase_kernel, kpoints, vectors),
        out_shape=jax.ShapeDtypeStruct((cores, vectors, 2 * order), F32),
        in_specs=[VMEM],
        out_specs=VMEM,
        scratch_shapes=[pltpu.VMEM((length, LANES), F32)],
        compiler_params=params(),
        name="phase_sum",
    )(arrived.reshape(length, LANES))
    parts = lax.all_to_all(parts, CORES, split_axis=0, concat_axis=0, tiled=True)

    host_rows, sent = pl.pallas_call(
        functools.partial(product_kernel, scale, slots),
        out_shape=(
            jax.ShapeDtypeStruct((2 * vectors, LANES), F32),
            jax.ShapeDtypeStruct((chips * slots * 4, LANES), BF16),
        ),
        in_specs=[VMEM, VMEM, VMEM],
        out_specs=(VMEM, VMEM),
        scratch_shapes=[
            pltpu.VMEM((chips * slots * 4, LANES), F32),
            pltpu.VMEM((4 * vectors, 2 * order), F32),
        ],
        compiler_params=params(),
        name="product",
    )(parts, delta_t, chosen)
    sent = sent.reshape(chips, slots * 4, LANES)
    got = lax.all_to_all(sent, CHIPS, split_axis=0, concat_axis=0, tiled=True)
    cluster = pl.pallas_call(
        place_kernel,
        out_shape=jax.ShapeDtypeStruct((slots, chips, 4, LANES), BF16),
        in_specs=[VMEM],
        out_specs=HBM,
        scratch_shapes=[pltpu.SemaphoreType.DMA((slots,))],
        compiler_params=params(),
        name="place",
    )(got.reshape(chips, slots, 4, LANES))
    return (host_rows, cluster.reshape(slots, order, LANES))


def solution(mesh):
    fine = Mesh(mesh.devices.reshape(8, 8, 2, 4), ("y", "z", "c", "pair"))
    ka = ("y", "z", "c")
    in_specs = (P(ka, None, None, None), P(ka, None), P(), P(), P(), P(), P())
    out_specs = (P(ka, "pair"), P(ka, None, "pair"))
    return jax.shard_map(
        per_device, mesh=fine, in_specs=in_specs, out_specs=out_specs, check_vma=False
    )
```

```python
import functools
import math

import jax
import jax.numpy as jnp
import numpy as np
from jax import lax
from jax.experimental import pallas as pl
from jax.experimental.pallas import tpu as pltpu
from jax.sharding import Mesh
from jax.sharding import PartitionSpec as P

ITERS = 6
KG = 16
LANES = 128
CHIPS = ("y", "z")
CORES = ("c", "pair")
F32 = jnp.float32
BF16 = jnp.bfloat16


def dot(a, b):
    return jnp.dot(a, b, preferred_element_type=F32)


def turn_tables():
    angles = np.arange(KG) * (2.0 * math.pi / KG)
    tables = []
    for values in (np.cos(angles), np.sin(angles)):
        values = values.astype(np.float32)
        high = values.astype(jnp.bfloat16).astype(np.float32)
        tables += [high, (values - high).astype(jnp.bfloat16).astype(np.float32)]
    return tables


def fetch(places, sems):
    copies = [
        pltpu.make_async_copy(start, end, sems.at[i]) for i, (start, end) in enumerate(places)
    ]
    for copy in copies:
        copy.start()
    return copies


def solve_kernel(
    kinds, grid_in, lattice_in, matrix_in, route_in, species_in, count_in, out, combo, *scratch
):
    grid, lattice, matrix, route, species, count, wide, sems = scratch
    kpoints, _, order, _ = matrix.shape
    own = order // 4
    chunk = out.shape[0] // own
    places = [(matrix_in.at[k, i], matrix.at[k, i]) for k in range(kpoints) for i in range(2)]
    places = [(grid_in, grid), (lattice_in, lattice)] + places
    places += [(route_in, route), (species_in, species), (count_in, count)]
    copies = fetch(places, sems)
    small, large, late = copies[:2], copies[2:-3], copies[-3:]
    for copy in small:
        copy.wait()
    vectors = lattice.shape[1]
    lane = lax.broadcasted_iota(jnp.int32, (8, LANES), 1)
    turn = jnp.zeros((8, LANES), jnp.int32)
    for r in range(vectors):
        for k in range(kpoints):
            m = (
                grid[k, 0] * lattice[0, r]
                + grid[k, 1] * lattice[1, r]
                + grid[k, 2] * lattice[2, r]
            ) & (KG - 1)
            here = ((lane // (4 * vectors)) == k) & ((lane & (vectors - 1)) == r)
            turn = jnp.where(here, m, turn)
    kind = (lane // vectors) & 3
    phase = jnp.zeros((8, LANES), F32)
    for which, table in enumerate(turn_tables()):
        for m in range(KG):
            phase = jnp.where((kind == which) & (turn == m), float(table[m]), phase)
    phase = jnp.broadcast_to(phase[:1], (own, LANES))
    wide[pl.ds(chunk - 2, own, stride=chunk), :] = phase
    wide[pl.ds(chunk - 1, own, stride=chunk), :] = jnp.zeros((own, LANES), F32)
    row = lax.broadcasted_iota(jnp.int32, (own, order), 0)
    col = lax.broadcasted_iota(jnp.int32, (own, order), 1)
    pick = jnp.where(col == row * 4 + lax.axis_index("pair"), 1.0, 0.0).astype(BF16)
    first = []
    for k in range(kpoints):
        large[2 * k].wait()
        large[2 * k + 1].wait()
        first.append([dot(pick, matrix[k, part]) for part in range(2)])
    now = [list(pair) for pair in first]
    for step in range(ITERS - 1):
        for k in range(kpoints):
            re, im = now[k]
            re_high, im_high = re.astype(BF16), im.astype(BF16)
            parts = [re_high, im_high]
            if step > 0:
                parts.append((re - re_high.astype(F32)).astype(BF16))
                parts.append((im - im_high.astype(F32)).astype(BF16))
            left = jnp.concatenate(parts, axis=0)
            u = dot(left, matrix[k, 0])
            v = dot(left, matrix[k, 1])
            if step > 0:
                u = u[: 2 * own] + u[2 * own :]
                v = v[: 2 * own] + v[2 * own :]
            now[k] = [
                first[k][0] + u[:own] - v[own:],
                first[k][1] + v[:own] + u[own:],
            ]
    for k in range(kpoints):
        for part in range(2):
            for half in range(order // LANES):
                place = (k * 2 + part) * (order // LANES) + half
                wide[pl.ds(place, own, stride=chunk), :] = now[k][part][
                    :, half * LANES : (half + 1) * LANES
                ]
    for copy in late:
        copy.wait()
    alive = lax.broadcasted_iota(jnp.int32, combo.shape, 0) < count[...]
    combo[...] = jnp.where(alive, species[...] * vectors + route[...], kinds * vectors)
    out[...] = wide[...].astype(BF16)


def phase_kernel(kpoints, vectors, rows, out, wide):
    chunk = 2 + 4 * kpoints
    sources = rows.shape[0] // chunk
    wide[...] = rows[...].astype(F32)
    info = wide[pl.ds(chunk - 2, sources, stride=chunk), :]
    info = jnp.transpose(info).astype(BF16)
    total = jnp.zeros((4 * vectors, 4 * LANES), F32)
    for k in range(kpoints):
        block = [wide[pl.ds(k * 4 + q, sources, stride=chunk), :] for q in range(4)]
        block = jnp.concatenate(block, axis=1).astype(BF16)
        total = total + dot(info[k * 4 * vectors : (k + 1) * 4 * vectors], block)
    cosine = total[:vectors] + total[vectors : 2 * vectors]
    sine = total[2 * vectors : 3 * vectors] + total[3 * vectors :]
    half = 2 * LANES
    re = cosine[:, :half] - sine[:, half:]
    im = cosine[:, half:] + sine[:, :half]
    both = jnp.concatenate([re, im], axis=1)
    out[...] = jnp.broadcast_to(both[None], out.shape)


def product_kernel(scale, parts, delta, combo, host, out, wide, sums, chosen):
    vectors = parts.shape[1]
    kinds, _, order, _ = delta.shape
    slots, owners = combo.shape
    pair, core = lax.axis_index("pair"), lax.axis_index("c")
    half = LANES // 2
    for q in range(4):
        sums[q * vectors : (q + 1) * vectors, :] = (parts[q] + parts[4 + q]) * scale
    odd = (pair & 1) == 1
    lane = lax.broadcasted_iota(jnp.int32, (1, LANES), 1)

    def window(re, im):
        re = jnp.where(odd, pltpu.roll(re, half, 1), re)
        im = jnp.where(odd, im, pltpu.roll(im, half, 1))
        return jnp.where(lane < half, re, im)

    own = pl.multiple_of(core * (2 * vectors), 2 * vectors)
    at = pl.multiple_of((pair // 2) * LANES, LANES)
    host[...] = window(
        sums[pl.ds(own, 2 * vectors), pl.ds(at, LANES)],
        sums[pl.ds(own, 2 * vectors), pl.ds(order + at, LANES)],
    )
    rows = 4 * vectors
    left = jnp.concatenate([sums[:, :order], sums[:, order:]], axis=0).astype(BF16)
    table = []
    for s in range(kinds):
        u = dot(left, delta[s, 0])
        v = dot(left, delta[s, 1])
        re = u[:rows] - v[rows:]
        im = v[:rows] + u[rows:]
        re = jnp.where(pair >= 2, re[:, LANES:], re[:, :LANES])
        im = jnp.where(pair >= 2, im[:, LANES:], im[:, :LANES])
        product = window(re, im)
        table.append(
            jnp.concatenate([product[q * vectors : (q + 1) * vectors] for q in range(4)], axis=1)
        )
    table = jnp.concatenate(table, axis=0).astype(BF16)
    combo = jnp.transpose(combo[...].astype(F32)).astype(BF16)
    chips = owners // 2
    row = lax.broadcasted_iota(jnp.int32, (chips, owners), 0)
    col = lax.broadcasted_iota(jnp.int32, (chips, owners), 1)
    combo = dot(jnp.where(col == row * 2 + core, 1.0, 0.0).astype(BF16), combo)
    kind = lax.broadcasted_iota(jnp.int32, (chips, LANES), 1).astype(F32)
    for t in range(slots):
        hit = jnp.broadcast_to(combo[:, t : t + 1], kind.shape) == kind
        chosen[pl.ds(t, chips, stride=slots), :] = jnp.where(hit, 1.0, 0.0)
    chosen = chosen[:, : kinds * vectors].astype(BF16)
    picked = dot(chosen, table)
    for q in range(4):
        wide[pl.ds(q, chips * slots, stride=4), :] = picked[:, q * LANES : (q + 1) * LANES]
    out[...] = wide[...].astype(BF16)


def place_kernel(got, out, sems):
    places = [(got.at[:, t], out.at[t]) for t in range(out.shape[0])]
    for copy in fetch(places, sems):
        copy.wait()


VMEM = pl.BlockSpec(memory_space=pltpu.VMEM)
SMEM = pl.BlockSpec(memory_space=pltpu.SMEM)
HBM = pl.BlockSpec(memory_space=pltpu.HBM)


def in_hbm(x):
    return pltpu.with_memory_space_constraint(x, pltpu.HBM)


def params():
    return pltpu.CompilerParams(vmem_limit_bytes=32 * 1024 * 1024)


def per_device(kkr_matrix, kpoint_grid, lattice, delta_t, pair_count, pair_route, species):
    chips = lax.axis_size(CHIPS)
    cores = lax.axis_size(CORES)
    order = kkr_matrix.shape[2]
    kpoints = kkr_matrix.shape[0]
    vectors = lattice.shape[0]
    slots = pair_route.shape[1]
    kinds = delta_t.shape[0]
    scale = math.sqrt(order / (kpoints * chips * lax.axis_size("c")))
    chunk = 4 * kpoints + 2
    length = chips * chunk

    route, kind, count = pair_route.T, species.T, pair_count[None]
    outgoing, combo = pl.pallas_call(
        functools.partial(solve_kernel, kinds),
        out_shape=(
            jax.ShapeDtypeStruct((length, LANES), BF16),
            jax.ShapeDtypeStruct(route.shape, jnp.int32),
        ),
        in_specs=[HBM] * 6,
        out_specs=(VMEM, VMEM),
        scratch_shapes=[
            pltpu.SMEM((kpoints, 3), jnp.int32),
            pltpu.SMEM((3, vectors), jnp.int32),
            pltpu.VMEM(kkr_matrix.shape, BF16),
            pltpu.VMEM(route.shape, jnp.int32),
            pltpu.VMEM(kind.shape, jnp.int32),
            pltpu.VMEM(count.shape, jnp.int32),
            pltpu.VMEM((length, LANES), F32),
            pltpu.SemaphoreType.DMA((2 * kpoints + 5,)),
        ],
        compiler_params=params(),
        name="solve",
    )(*map(in_hbm, (kpoint_grid, lattice.T, kkr_matrix, route, kind, count)))
    outgoing = outgoing.reshape(chips, chunk // 2, 2, LANES)
    arrived = lax.all_to_all(outgoing, CHIPS, split_axis=0, concat_axis=0, tiled=True)

    parts = pl.pallas_call(
        functools.partial(phase_kernel, kpoints, vectors),
        out_shape=jax.ShapeDtypeStruct((cores, vectors, 2 * order), F32),
        in_specs=[VMEM],
        out_specs=VMEM,
        scratch_shapes=[pltpu.VMEM((length, LANES), F32)],
        compiler_params=params(),
        name="phase_sum",
    )(arrived.reshape(length, LANES))
    parts = lax.all_to_all(parts, CORES, split_axis=0, concat_axis=0, tiled=True)

    host_rows, sent = pl.pallas_call(
        functools.partial(product_kernel, scale),
        out_shape=(
            jax.ShapeDtypeStruct((2 * vectors, LANES), F32),
            jax.ShapeDtypeStruct((chips * slots * 4, LANES), BF16),
        ),
        in_specs=[VMEM, VMEM, VMEM],
        out_specs=(VMEM, VMEM),
        scratch_shapes=[
            pltpu.VMEM((chips * slots * 4, LANES), F32),
            pltpu.VMEM((4 * vectors, 2 * order), F32),
            pltpu.VMEM((chips * slots, LANES), F32),
        ],
        compiler_params=params(),
        name="product",
    )(parts, delta_t, combo)
    sent = sent.reshape(chips, slots * 4, LANES)
    got = lax.all_to_all(sent, CHIPS, split_axis=0, concat_axis=0, tiled=True)
    cluster = pl.pallas_call(
        place_kernel,
        out_shape=jax.ShapeDtypeStruct((slots, chips, 4, LANES), BF16),
        in_specs=[VMEM],
        out_specs=HBM,
        scratch_shapes=[pltpu.SemaphoreType.DMA((slots,))],
        compiler_params=params(),
        name="place",
    )(got.reshape(chips, slots, 4, LANES))
    return (host_rows, cluster.reshape(slots, order, LANES))


def solution(mesh):
    fine = Mesh(mesh.devices.reshape(8, 8, 2, 4), ("y", "z", "c", "pair"))
    ka = ("y", "z", "c")
    in_specs = (P(ka, None, None, None), P(ka, None), P(), P(), P(), P(), P())
    out_specs = (P(ka, "pair"), P(ka, None, "pair"))
    return jax.shard_map(
        per_device, mesh=fine, in_specs=in_specs, out_specs=out_specs, check_vma=False
    )
```

```python
import functools
import math

import jax
import jax.numpy as jnp
import numpy as np
from jax import lax
from jax.experimental import pallas as pl
from jax.experimental.pallas import tpu as pltpu
from jax.sharding import Mesh
from jax.sharding import PartitionSpec as P

ITERS = 6
KG = 16
LANES = 128
CHIPS = ("y", "z")
CORES = ("c", "pair")
F32 = jnp.float32
BF16 = jnp.bfloat16


def dot(a, b):
    return jnp.dot(a, b, preferred_element_type=F32)


def turn_tables():
    angles = np.arange(KG) * (2.0 * math.pi / KG)
    tables = []
    for values in (np.cos(angles), np.sin(angles)):
        values = values.astype(np.float32)
        high = values.astype(jnp.bfloat16).astype(np.float32)
        tables += [high, (values - high).astype(jnp.bfloat16).astype(np.float32)]
    return tables


def fetch(places, sems):
    copies = [
        pltpu.make_async_copy(start, end, sems.at[i]) for i, (start, end) in enumerate(places)
    ]
    for copy in copies:
        copy.start()
    return copies


def solve_kernel(
    kinds, grid_in, lattice_in, matrix_in, route_in, species_in, count_in, out, combo, *scratch
):
    grid, lattice, matrix, route, species, count, wide, sems = scratch
    kpoints, _, order, _ = matrix.shape
    own = order // 4
    chunk = out.shape[0] // own
    places = [
        (matrix_in.at[k, i, j : j + order // 2], matrix.at[k, i, j : j + order // 2])
        for k in range(kpoints)
        for i in range(2)
        for j in (0, order // 2)
    ]
    places = [(grid_in, grid), (lattice_in, lattice)] + places
    places += [(route_in, route), (species_in, species), (count_in, count)]
    copies = fetch(places, sems)
    small, large, late = copies[:2], copies[2:-3], copies[-3:]
    for copy in small:
        copy.wait()
    vectors = lattice.shape[1]
    lane = lax.broadcasted_iota(jnp.int32, (8, LANES), 1)
    turn = jnp.zeros((8, LANES), jnp.int32)
    for r in range(vectors):
        for k in range(kpoints):
            m = (
                grid[k, 0] * lattice[0, r]
                + grid[k, 1] * lattice[1, r]
                + grid[k, 2] * lattice[2, r]
            ) & (KG - 1)
            here = ((lane // (4 * vectors)) == k) & ((lane & (vectors - 1)) == r)
            turn = jnp.where(here, m, turn)
    kind = (lane // vectors) & 3
    phase = jnp.zeros((8, LANES), F32)
    for which, table in enumerate(turn_tables()):
        for m in range(KG):
            phase = jnp.where((kind == which) & (turn == m), float(table[m]), phase)
    phase = jnp.broadcast_to(phase[:1], (own, LANES))
    wide[pl.ds(chunk - 2, own, stride=chunk), :] = phase
    wide[pl.ds(chunk - 1, own, stride=chunk), :] = jnp.zeros((own, LANES), F32)
    row = lax.broadcasted_iota(jnp.int32, (own, order), 0)
    col = lax.broadcasted_iota(jnp.int32, (own, order), 1)
    pick = jnp.where(col == row * 4 + lax.axis_index("pair"), 1.0, 0.0).astype(BF16)
    first = []
    for k in range(kpoints):
        for copy in large[4 * k : 4 * k + 4]:
            copy.wait()
        first.append([dot(pick, matrix[k, part]) for part in range(2)])
    now = [list(pair) for pair in first]
    for step in range(ITERS - 1):
        for k in range(kpoints):
            re, im = now[k]
            re_high, im_high = re.astype(BF16), im.astype(BF16)
            parts = [re_high, im_high]
            if step > 0:
                parts.append((re - re_high.astype(F32)).astype(BF16))
                parts.append((im - im_high.astype(F32)).astype(BF16))
            left = jnp.concatenate(parts, axis=0)
            u = dot(left, matrix[k, 0])
            v = dot(left, matrix[k, 1])
            if step > 0:
                u = u[: 2 * own] + u[2 * own :]
                v = v[: 2 * own] + v[2 * own :]
            now[k] = [
                first[k][0] + u[:own] - v[own:],
                first[k][1] + v[:own] + u[own:],
            ]
    for k in range(kpoints):
        for part in range(2):
            for half in range(order // LANES):
                place = (k * 2 + part) * (order // LANES) + half
                wide[pl.ds(place, own, stride=chunk), :] = now[k][part][
                    :, half * LANES : (half + 1) * LANES
                ]
    for copy in late:
        copy.wait()
    alive = lax.broadcasted_iota(jnp.int32, combo.shape, 0) < count[...]
    combo[...] = jnp.where(alive, species[...] * vectors + route[...], kinds * vectors)
    out[...] = wide[...].astype(BF16)


def phase_kernel(kpoints, vectors, rows, out, wide):
    chunk = 2 + 4 * kpoints
    sources = rows.shape[0] // chunk
    wide[...] = rows[...].astype(F32)
    info = wide[pl.ds(chunk - 2, sources, stride=chunk), :]
    info = jnp.transpose(info).astype(BF16)
    total = jnp.zeros((4 * vectors, 4 * LANES), F32)
    for k in range(kpoints):
        block = [wide[pl.ds(k * 4 + q, sources, stride=chunk), :] for q in range(4)]
        block = jnp.concatenate(block, axis=1).astype(BF16)
        total = total + dot(info[k * 4 * vectors : (k + 1) * 4 * vectors], block)
    cosine = total[:vectors] + total[vectors : 2 * vectors]
    sine = total[2 * vectors : 3 * vectors] + total[3 * vectors :]
    half = 2 * LANES
    re = cosine[:, :half] - sine[:, half:]
    im = cosine[:, half:] + sine[:, :half]
    both = jnp.concatenate([re, im], axis=1).astype(BF16)
    out[...] = jnp.broadcast_to(both[None], out.shape)


def product_kernel(scale, parts, delta, combo, host, out, wide, sums, chosen):
    vectors = parts.shape[1]
    kinds, _, order, _ = delta.shape
    slots, owners = combo.shape
    pair, core = lax.axis_index("pair"), lax.axis_index("c")
    half = LANES // 2
    for q in range(4):
        sums[q * vectors : (q + 1) * vectors, :] = (
            parts[q].astype(F32) + parts[4 + q].astype(F32)
        ) * scale
    odd = (pair & 1) == 1
    lane = lax.broadcasted_iota(jnp.int32, (1, LANES), 1)

    def window(re, im):
        re = jnp.where(odd, pltpu.roll(re, half, 1), re)
        im = jnp.where(odd, im, pltpu.roll(im, half, 1))
        return jnp.where(lane < half, re, im)

    own = pl.multiple_of(core * (2 * vectors), 2 * vectors)
    at = pl.multiple_of((pair // 2) * LANES, LANES)
    host[...] = window(
        sums[pl.ds(own, 2 * vectors), pl.ds(at, LANES)],
        sums[pl.ds(own, 2 * vectors), pl.ds(order + at, LANES)],
    )
    rows = 4 * vectors
    left = jnp.concatenate([sums[:, :order], sums[:, order:]], axis=0).astype(BF16)
    table = []
    for s in range(kinds):
        u = dot(left, delta[s, 0])
        v = dot(left, delta[s, 1])
        re = u[:rows] - v[rows:]
        im = v[:rows] + u[rows:]
        re = jnp.where(pair >= 2, re[:, LANES:], re[:, :LANES])
        im = jnp.where(pair >= 2, im[:, LANES:], im[:, :LANES])
        product = window(re, im)
        table.append(
            jnp.concatenate([product[q * vectors : (q + 1) * vectors] for q in range(4)], axis=1)
        )
    table = jnp.concatenate(table, axis=0).astype(BF16)
    combo = jnp.transpose(combo[...].astype(F32)).astype(BF16)
    chips = owners // 2
    row = lax.broadcasted_iota(jnp.int32, (chips, owners), 0)
    col = lax.broadcasted_iota(jnp.int32, (chips, owners), 1)
    combo = dot(jnp.where(col == row * 2 + core, 1.0, 0.0).astype(BF16), combo)
    kind = lax.broadcasted_iota(jnp.int32, (chips, LANES), 1).astype(F32)
    for t in range(slots):
        hit = jnp.broadcast_to(combo[:, t : t + 1], kind.shape) == kind
        chosen[pl.ds(t, chips, stride=slots), :] = jnp.where(hit, 1.0, 0.0)
    chosen = chosen[:, : kinds * vectors].astype(BF16)
    picked = dot(chosen, table)
    for q in range(4):
        wide[pl.ds(q, chips * slots, stride=4), :] = picked[:, q * LANES : (q + 1) * LANES]
    out[...] = wide[...].astype(BF16)


def place_kernel(got, out, sems):
    places = [(got.at[:, t], out.at[t]) for t in range(out.shape[0])]
    for copy in fetch(places, sems):
        copy.wait()


VMEM = pl.BlockSpec(memory_space=pltpu.VMEM)
SMEM = pl.BlockSpec(memory_space=pltpu.SMEM)
HBM = pl.BlockSpec(memory_space=pltpu.HBM)


def in_hbm(x):
    return pltpu.with_memory_space_constraint(x, pltpu.HBM)


def params():
    return pltpu.CompilerParams(vmem_limit_bytes=32 * 1024 * 1024)


def per_device(kkr_matrix, kpoint_grid, lattice, delta_t, pair_count, pair_route, species):
    chips = lax.axis_size(CHIPS)
    cores = lax.axis_size(CORES)
    order = kkr_matrix.shape[2]
    kpoints = kkr_matrix.shape[0]
    vectors = lattice.shape[0]
    slots = pair_route.shape[1]
    kinds = delta_t.shape[0]
    scale = math.sqrt(order / (kpoints * chips * lax.axis_size("c")))
    chunk = 4 * kpoints + 2
    length = chips * chunk

    route, kind, count = pair_route.T, species.T, pair_count[None]
    outgoing, combo = pl.pallas_call(
        functools.partial(solve_kernel, kinds),
        out_shape=(
            jax.ShapeDtypeStruct((length, LANES), BF16),
            jax.ShapeDtypeStruct(route.shape, jnp.int32),
        ),
        in_specs=[HBM] * 6,
        out_specs=(VMEM, VMEM),
        scratch_shapes=[
            pltpu.SMEM((kpoints, 3), jnp.int32),
            pltpu.SMEM((3, vectors), jnp.int32),
            pltpu.VMEM(kkr_matrix.shape, BF16),
            pltpu.VMEM(route.shape, jnp.int32),
            pltpu.VMEM(kind.shape, jnp.int32),
            pltpu.VMEM(count.shape, jnp.int32),
            pltpu.VMEM((length, LANES), F32),
            pltpu.SemaphoreType.DMA((4 * kpoints + 5,)),
        ],
        compiler_params=params(),
        name="solve",
    )(*map(in_hbm, (kpoint_grid, lattice.T, kkr_matrix, route, kind, count)))
    outgoing = outgoing.reshape(chips, chunk // 2, 2, LANES)
    arrived = lax.all_to_all(outgoing, CHIPS, split_axis=0, concat_axis=0, tiled=True)

    parts = pl.pallas_call(
        functools.partial(phase_kernel, kpoints, vectors),
        out_shape=jax.ShapeDtypeStruct((cores, vectors, 2 * order), BF16),
        in_specs=[VMEM],
        out_specs=VMEM,
        scratch_shapes=[pltpu.VMEM((length, LANES), F32)],
        compiler_params=params(),
        name="phase_sum",
    )(arrived.reshape(length, LANES))
    parts = lax.all_to_all(parts, CORES, split_axis=0, concat_axis=0, tiled=True)

    host_rows, sent = pl.pallas_call(
        functools.partial(product_kernel, scale),
        out_shape=(
            jax.ShapeDtypeStruct((2 * vectors, LANES), F32),
            jax.ShapeDtypeStruct((chips * slots * 4, LANES), BF16),
        ),
        in_specs=[VMEM, VMEM, VMEM],
        out_specs=(VMEM, VMEM),
        scratch_shapes=[
            pltpu.VMEM((chips * slots * 4, LANES), F32),
            pltpu.VMEM((4 * vectors, 2 * order), F32),
            pltpu.VMEM((chips * slots, LANES), F32),
        ],
        compiler_params=params(),
        name="product",
    )(parts, delta_t, combo)
    sent = sent.reshape(chips, slots * 4, LANES)
    got = lax.all_to_all(sent, CHIPS, split_axis=0, concat_axis=0, tiled=True)
    cluster = pl.pallas_call(
        place_kernel,
        out_shape=jax.ShapeDtypeStruct((slots, chips, 4, LANES), BF16),
        in_specs=[VMEM],
        out_specs=HBM,
        scratch_shapes=[pltpu.SemaphoreType.DMA((slots,))],
        compiler_params=params(),
        name="place",
    )(got.reshape(chips, slots, 4, LANES))
    return (host_rows, cluster.reshape(slots, order, LANES))


def solution(mesh):
    fine = Mesh(mesh.devices.reshape(8, 8, 2, 4), ("y", "z", "c", "pair"))
    ka = ("y", "z", "c")
    in_specs = (P(ka, None, None, None), P(ka, None), P(), P(), P(), P(), P())
    out_specs = (P(ka, "pair"), P(ka, None, "pair"))
    return jax.shard_map(
        per_device, mesh=fine, in_specs=in_specs, out_specs=out_specs, check_vma=False
    )
```

```python
import functools
import math

import jax
import jax.numpy as jnp
import numpy as np
from jax import lax
from jax.experimental import pallas as pl
from jax.experimental.pallas import tpu as pltpu
from jax.sharding import Mesh
from jax.sharding import PartitionSpec as P

ITERS = 6
KG = 16
LANES = 128
CHIPS = ("y", "z")
CORES = ("c", "pair")
F32 = jnp.float32
BF16 = jnp.bfloat16


def dot(a, b):
    return jnp.dot(a, b, preferred_element_type=F32)


def turn_tables():
    angles = np.arange(KG) * (2.0 * math.pi / KG)
    tables = []
    for values in (np.cos(angles), np.sin(angles)):
        values = values.astype(np.float32)
        high = values.astype(jnp.bfloat16).astype(np.float32)
        tables += [high, (values - high).astype(jnp.bfloat16).astype(np.float32)]
    return tables


def fetch(places, sems):
    copies = [
        pltpu.make_async_copy(start, end, sems.at[i]) for i, (start, end) in enumerate(places)
    ]
    for copy in copies:
        copy.start()
    return copies


def solve_kernel(
    kinds, grid_in, lattice_in, matrix_in, route_in, species_in, count_in, out, combo, *scratch
):
    grid, lattice, matrix, route, species, count, wide, sems = scratch
    kpoints, _, order, _ = matrix.shape
    own = order // 4
    chunk = out.shape[0] // own
    places = [(matrix_in.at[k, i], matrix.at[k, i]) for k in range(kpoints) for i in range(2)]
    places = [(grid_in, grid), (lattice_in, lattice)] + places
    places += [(route_in, route), (species_in, species), (count_in, count)]
    copies = fetch(places, sems)
    small, large, late = copies[:2], copies[2:-3], copies[-3:]
    for copy in small:
        copy.wait()
    vectors = lattice.shape[1]
    lane = lax.broadcasted_iota(jnp.int32, (8, LANES), 1)
    turn = jnp.zeros((8, LANES), jnp.int32)
    for r in range(vectors):
        for k in range(kpoints):
            m = (
                grid[k, 0] * lattice[0, r]
                + grid[k, 1] * lattice[1, r]
                + grid[k, 2] * lattice[2, r]
            ) & (KG - 1)
            here = ((lane // (4 * vectors)) == k) & ((lane & (vectors - 1)) == r)
            turn = jnp.where(here, m, turn)
    kind = (lane // vectors) & 3
    phase = jnp.zeros((8, LANES), F32)
    for which, table in enumerate(turn_tables()):
        for m in range(KG):
            phase = jnp.where((kind == which) & (turn == m), float(table[m]), phase)
    phase = jnp.broadcast_to(phase[:1], (own, LANES))
    wide[pl.ds(chunk - 2, own, stride=chunk), :] = phase
    wide[pl.ds(chunk - 1, own, stride=chunk), :] = jnp.zeros((own, LANES), F32)
    row = lax.broadcasted_iota(jnp.int32, (own, order), 0)
    col = lax.broadcasted_iota(jnp.int32, (own, order), 1)
    pick = jnp.where(col == row * 4 + lax.axis_index("pair"), 1.0, 0.0).astype(BF16)
    first = []
    for k in range(kpoints):
        large[2 * k].wait()
        large[2 * k + 1].wait()
        first.append([dot(pick, matrix[k, part]) for part in range(2)])
    now = [list(pair) for pair in first]
    for step in range(ITERS - 1):
        for k in range(kpoints):
            re, im = now[k]
            re_high, im_high = re.astype(BF16), im.astype(BF16)
            parts = [re_high, im_high]
            if step > 0:
                parts.append((re - re_high.astype(F32)).astype(BF16))
                parts.append((im - im_high.astype(F32)).astype(BF16))
            left = jnp.concatenate(parts, axis=0)
            u = dot(left, matrix[k, 0])
            v = dot(left, matrix[k, 1])
            if step > 0:
                u = u[: 2 * own] + u[2 * own :]
                v = v[: 2 * own] + v[2 * own :]
            now[k] = [
                first[k][0] + u[:own] - v[own:],
                first[k][1] + v[:own] + u[own:],
            ]
    for k in range(kpoints):
        for part in range(2):
            for half in range(order // LANES):
                place = (k * 2 + part) * (order // LANES) + half
                wide[pl.ds(place, own, stride=chunk), :] = now[k][part][
                    :, half * LANES : (half + 1) * LANES
                ]
    for copy in late:
        copy.wait()
    alive = lax.broadcasted_iota(jnp.int32, combo.shape, 0) < count[...]
    combo[...] = jnp.where(alive, species[...] * vectors + route[...], kinds * vectors)
    out[...] = wide[...].astype(BF16)


def phase_kernel(kpoints, vectors, rows, out, wide):
    chunk = 2 + 4 * kpoints
    sources = rows.shape[0] // chunk
    wide[...] = rows[...].astype(F32)
    info = wide[pl.ds(chunk - 2, sources, stride=chunk), :]
    info = jnp.transpose(info).astype(BF16)
    total = jnp.zeros((4 * vectors, 4 * LANES), F32)
    for k in range(kpoints):
        block = [wide[pl.ds(k * 4 + q, sources, stride=chunk), :] for q in range(4)]
        block = jnp.concatenate(block, axis=1).astype(BF16)
        total = total + dot(info[k * 4 * vectors : (k + 1) * 4 * vectors], block)
    cosine = total[:vectors] + total[vectors : 2 * vectors]
    sine = total[2 * vectors : 3 * vectors] + total[3 * vectors :]
    half = 2 * LANES
    re = cosine[:, :half] - sine[:, half:]
    im = cosine[:, half:] + sine[:, :half]
    both = jnp.concatenate([re, im], axis=1).astype(BF16)
    out[...] = jnp.broadcast_to(both[None], out.shape)


def product_kernel(scale, parts, delta, combo, host, out, wide, sums, chosen):
    vectors = parts.shape[1]
    kinds, _, order, _ = delta.shape
    slots, owners = combo.shape
    pair, core = lax.axis_index("pair"), lax.axis_index("c")
    half = LANES // 2
    for q in range(4):
        sums[q * vectors : (q + 1) * vectors, :] = (
            parts[q].astype(F32) + parts[4 + q].astype(F32)
        ) * scale
    odd = (pair & 1) == 1
    lane = lax.broadcasted_iota(jnp.int32, (1, LANES), 1)

    def window(re, im):
        re = jnp.where(odd, pltpu.roll(re, half, 1), re)
        im = jnp.where(odd, im, pltpu.roll(im, half, 1))
        return jnp.where(lane < half, re, im)

    own = pl.multiple_of(core * (2 * vectors), 2 * vectors)
    at = pl.multiple_of((pair // 2) * LANES, LANES)
    host[...] = window(
        sums[pl.ds(own, 2 * vectors), pl.ds(at, LANES)],
        sums[pl.ds(own, 2 * vectors), pl.ds(order + at, LANES)],
    )
    rows = 4 * vectors
    left = jnp.concatenate([sums[:, :order], sums[:, order:]], axis=0).astype(BF16)
    table = []
    for s in range(kinds):
        u = dot(left, delta[s, 0])
        v = dot(left, delta[s, 1])
        re = u[:rows] - v[rows:]
        im = v[:rows] + u[rows:]
        re = jnp.where(pair >= 2, re[:, LANES:], re[:, :LANES])
        im = jnp.where(pair >= 2, im[:, LANES:], im[:, :LANES])
        product = window(re, im)
        table.append(
            jnp.concatenate([product[q * vectors : (q + 1) * vectors] for q in range(4)], axis=1)
        )
    table = jnp.concatenate(table, axis=0).astype(BF16)
    combo = jnp.transpose(combo[...].astype(F32)).astype(BF16)
    chips = owners // 2
    row = lax.broadcasted_iota(jnp.int32, (chips, owners), 0)
    col = lax.broadcasted_iota(jnp.int32, (chips, owners), 1)
    combo = dot(jnp.where(col == row * 2 + core, 1.0, 0.0).astype(BF16), combo)
    kind = lax.broadcasted_iota(jnp.int32, (chips, LANES), 1).astype(F32)
    for t in range(slots):
        hit = jnp.broadcast_to(combo[:, t : t + 1], kind.shape) == kind
        chosen[pl.ds(t, chips, stride=slots), :] = jnp.where(hit, 1.0, 0.0)
    chosen = chosen[:, : kinds * vectors].astype(BF16)
    picked = dot(chosen, table)
    for q in range(4):
        wide[pl.ds(q, chips * slots, stride=4), :] = picked[:, q * LANES : (q + 1) * LANES]
    out[...] = wide[...].astype(BF16)


def place_kernel(got, out, sems):
    places = [(got.at[:, t], out.at[t]) for t in range(out.shape[0])]
    for copy in fetch(places, sems):
        copy.wait()


VMEM = pl.BlockSpec(memory_space=pltpu.VMEM)
SMEM = pl.BlockSpec(memory_space=pltpu.SMEM)
HBM = pl.BlockSpec(memory_space=pltpu.HBM)


def in_hbm(x):
    return pltpu.with_memory_space_constraint(x, pltpu.HBM)


def params():
    return pltpu.CompilerParams(vmem_limit_bytes=32 * 1024 * 1024)


def per_device(kkr_matrix, kpoint_grid, lattice, delta_t, pair_count, pair_route, species):
    chips = lax.axis_size(CHIPS)
    cores = lax.axis_size(CORES)
    order = kkr_matrix.shape[2]
    kpoints = kkr_matrix.shape[0]
    vectors = lattice.shape[0]
    slots = pair_route.shape[1]
    kinds = delta_t.shape[0]
    scale = math.sqrt(order / (kpoints * chips * lax.axis_size("c")))
    chunk = 4 * kpoints + 2
    length = chips * chunk

    route, kind, count = pair_route.T, species.T, pair_count[None]
    outgoing, combo = pl.pallas_call(
        functools.partial(solve_kernel, kinds),
        out_shape=(
            jax.ShapeDtypeStruct((length, LANES), BF16),
            jax.ShapeDtypeStruct(route.shape, jnp.int32),
        ),
        in_specs=[HBM] * 6,
        out_specs=(VMEM, VMEM),
        scratch_shapes=[
            pltpu.SMEM((kpoints, 3), jnp.int32),
            pltpu.SMEM((3, vectors), jnp.int32),
            pltpu.VMEM(kkr_matrix.shape, BF16),
            pltpu.VMEM(route.shape, jnp.int32),
            pltpu.VMEM(kind.shape, jnp.int32),
            pltpu.VMEM(count.shape, jnp.int32),
            pltpu.VMEM((length, LANES), F32),
            pltpu.SemaphoreType.DMA((2 * kpoints + 5,)),
        ],
        compiler_params=params(),
        name="solve",
    )(*map(in_hbm, (kpoint_grid, lattice.T, kkr_matrix, route, kind, count)))
    outgoing = outgoing.reshape(chips, chunk // 2, 2, LANES)
    arrived = lax.all_to_all(outgoing, CHIPS, split_axis=0, concat_axis=0, tiled=True)

    parts = pl.pallas_call(
        functools.partial(phase_kernel, kpoints, vectors),
        out_shape=jax.ShapeDtypeStruct((cores, vectors, 2 * order), BF16),
        in_specs=[VMEM],
        out_specs=VMEM,
        scratch_shapes=[pltpu.VMEM((length, LANES), F32)],
        compiler_params=params(),
        name="phase_sum",
    )(arrived.reshape(length, LANES))
    parts = lax.all_to_all(parts, CORES, split_axis=0, concat_axis=0, tiled=True)

    host_rows, sent = pl.pallas_call(
        functools.partial(product_kernel, scale),
        out_shape=(
            jax.ShapeDtypeStruct((2 * vectors, LANES), F32),
            jax.ShapeDtypeStruct((chips * slots * 4, LANES), BF16),
        ),
        in_specs=[VMEM, VMEM, VMEM],
        out_specs=(VMEM, VMEM),
        scratch_shapes=[
            pltpu.VMEM((chips * slots * 4, LANES), F32),
            pltpu.VMEM((4 * vectors, 2 * order), F32),
            pltpu.VMEM((chips * slots, LANES), F32),
        ],
        compiler_params=params(),
        name="product",
    )(parts, delta_t, combo)
    sent = sent.reshape(chips, slots * 4, LANES)
    got = lax.all_to_all(sent, CHIPS, split_axis=0, concat_axis=0, tiled=True)
    cluster = pl.pallas_call(
        place_kernel,
        out_shape=jax.ShapeDtypeStruct((slots, chips, 4, LANES), BF16),
        in_specs=[VMEM],
        out_specs=HBM,
        scratch_shapes=[pltpu.SemaphoreType.DMA((slots,))],
        compiler_params=params(),
        name="place",
    )(got.reshape(chips, slots, 4, LANES))
    return (host_rows, cluster.reshape(slots, order, LANES))


def solution(mesh):
    fine = Mesh(mesh.devices.reshape(8, 8, 2, 4), ("y", "z", "c", "pair"))
    ka = ("y", "z", "c")
    in_specs = (P(ka, None, None, None), P(ka, None), P(), P(), P(), P(), P())
    out_specs = (P(ka, "pair"), P(ka, None, "pair"))
    return jax.shard_map(
        per_device, mesh=fine, in_specs=in_specs, out_specs=out_specs, check_vma=False
    )
```

```python
import functools
import math

import jax
import jax.numpy as jnp
import numpy as np
from jax import lax
from jax.experimental import pallas as pl
from jax.experimental.pallas import tpu as pltpu
from jax.sharding import Mesh
from jax.sharding import PartitionSpec as P

ITERS = 6
KG = 16
LANES = 128
CHIPS = ("y", "z")
CORES = ("c", "pair")
F32 = jnp.float32
BF16 = jnp.bfloat16


def dot(a, b):
    return jnp.dot(a, b, preferred_element_type=F32)


def turn_tables():
    angles = np.arange(KG) * (2.0 * math.pi / KG)
    tables = []
    for values in (np.cos(angles), np.sin(angles)):
        values = values.astype(np.float32)
        high = values.astype(jnp.bfloat16).astype(np.float32)
        tables += [high, (values - high).astype(jnp.bfloat16).astype(np.float32)]
    return tables


def fetch(places, sems):
    copies = [
        pltpu.make_async_copy(start, end, sems.at[i]) for i, (start, end) in enumerate(places)
    ]
    for copy in copies:
        copy.start()
    return copies


def solve_kernel(
    kinds, grid_in, lattice_in, matrix_in, route_in, species_in, count_in, out, combo, *scratch
):
    grid, lattice, matrix, route, species, count, wide, sems = scratch
    kpoints, _, order, _ = matrix.shape
    own = order // 4
    chunk = out.shape[0] // own
    places = [(matrix_in.at[k], matrix.at[k]) for k in range(kpoints)]
    places = [(grid_in, grid), (lattice_in, lattice)] + places
    places += [(route_in, route), (species_in, species), (count_in, count)]
    copies = fetch(places, sems)
    small, large, late = copies[:2], copies[2:-3], copies[-3:]
    for copy in small:
        copy.wait()
    vectors = lattice.shape[1]
    lane = lax.broadcasted_iota(jnp.int32, (8, LANES), 1)
    turn = jnp.zeros((8, LANES), jnp.int32)
    for r in range(vectors):
        for k in range(kpoints):
            m = (
                grid[k, 0] * lattice[0, r]
                + grid[k, 1] * lattice[1, r]
                + grid[k, 2] * lattice[2, r]
            ) & (KG - 1)
            here = ((lane // (4 * vectors)) == k) & ((lane & (vectors - 1)) == r)
            turn = jnp.where(here, m, turn)
    kind = (lane // vectors) & 3
    phase = jnp.zeros((8, LANES), F32)
    for which, table in enumerate(turn_tables()):
        for m in range(KG):
            phase = jnp.where((kind == which) & (turn == m), float(table[m]), phase)
    phase = jnp.broadcast_to(phase[:1], (own, LANES))
    wide[pl.ds(chunk - 2, own, stride=chunk), :] = phase
    wide[pl.ds(chunk - 1, own, stride=chunk), :] = jnp.zeros((own, LANES), F32)
    row = lax.broadcasted_iota(jnp.int32, (own, order), 0)
    col = lax.broadcasted_iota(jnp.int32, (own, order), 1)
    pick = jnp.where(col == row * 4 + lax.axis_index("pair"), 1.0, 0.0).astype(BF16)
    first = []
    for k in range(kpoints):
        large[k].wait()
        first.append([dot(pick, matrix[k, part]) for part in range(2)])
    now = [list(pair) for pair in first]
    for step in range(ITERS - 1):
        for k in range(kpoints):
            re, im = now[k]
            re_high, im_high = re.astype(BF16), im.astype(BF16)
            parts = [re_high, im_high]
            if step > 0:
                parts.append((re - re_high.astype(F32)).astype(BF16))
                parts.append((im - im_high.astype(F32)).astype(BF16))
            left = jnp.concatenate(parts, axis=0)
            u = dot(left, matrix[k, 0])
            v = dot(left, matrix[k, 1])
            if step > 0:
                u = u[: 2 * own] + u[2 * own :]
                v = v[: 2 * own] + v[2 * own :]
            now[k] = [
                first[k][0] + u[:own] - v[own:],
                first[k][1] + v[:own] + u[own:],
            ]
    for k in range(kpoints):
        for part in range(2):
            for half in range(order // LANES):
                place = (k * 2 + part) * (order // LANES) + half
                wide[pl.ds(place, own, stride=chunk), :] = now[k][part][
                    :, half * LANES : (half + 1) * LANES
                ]
    for copy in late:
        copy.wait()
    alive = lax.broadcasted_iota(jnp.int32, combo.shape, 0) < count[...]
    combo[...] = jnp.where(alive, species[...] * vectors + route[...], kinds * vectors)
    out[...] = wide[...].astype(BF16)


def phase_kernel(kpoints, vectors, rows, out, wide):
    chunk = 2 + 4 * kpoints
    sources = rows.shape[0] // chunk
    wide[...] = rows[...].astype(F32)
    info = wide[pl.ds(chunk - 2, sources, stride=chunk), :]
    info = jnp.transpose(info).astype(BF16)
    total = jnp.zeros((4 * vectors, 4 * LANES), F32)
    for k in range(kpoints):
        block = [wide[pl.ds(k * 4 + q, sources, stride=chunk), :] for q in range(4)]
        block = jnp.concatenate(block, axis=1).astype(BF16)
        total = total + dot(info[k * 4 * vectors : (k + 1) * 4 * vectors], block)
    cosine = total[:vectors] + total[vectors : 2 * vectors]
    sine = total[2 * vectors : 3 * vectors] + total[3 * vectors :]
    half = 2 * LANES
    re = cosine[:, :half] - sine[:, half:]
    im = cosine[:, half:] + sine[:, :half]
    both = jnp.concatenate([re, im], axis=1).astype(BF16)
    out[...] = jnp.broadcast_to(both[None], out.shape)


def product_kernel(scale, parts, delta, combo, host, out, wide, sums, chosen):
    vectors = parts.shape[1]
    kinds, _, order, _ = delta.shape
    slots, owners = combo.shape
    pair, core = lax.axis_index("pair"), lax.axis_index("c")
    half = LANES // 2
    for q in range(4):
        sums[q * vectors : (q + 1) * vectors, :] = (
            parts[q].astype(F32) + parts[4 + q].astype(F32)
        ) * scale
    odd = (pair & 1) == 1
    lane = lax.broadcasted_iota(jnp.int32, (1, LANES), 1)

    def window(re, im):
        re = jnp.where(odd, pltpu.roll(re, half, 1), re)
        im = jnp.where(odd, im, pltpu.roll(im, half, 1))
        return jnp.where(lane < half, re, im)

    own = pl.multiple_of(core * (2 * vectors), 2 * vectors)
    at = pl.multiple_of((pair // 2) * LANES, LANES)
    host[...] = window(
        sums[pl.ds(own, 2 * vectors), pl.ds(at, LANES)],
        sums[pl.ds(own, 2 * vectors), pl.ds(order + at, LANES)],
    )
    rows = 4 * vectors
    left = jnp.concatenate([sums[:, :order], sums[:, order:]], axis=0).astype(BF16)
    table = []
    for s in range(kinds):
        u = dot(left, delta[s, 0])
        v = dot(left, delta[s, 1])
        re = u[:rows] - v[rows:]
        im = v[:rows] + u[rows:]
        re = jnp.where(pair >= 2, re[:, LANES:], re[:, :LANES])
        im = jnp.where(pair >= 2, im[:, LANES:], im[:, :LANES])
        product = window(re, im)
        table.append(
            jnp.concatenate([product[q * vectors : (q + 1) * vectors] for q in range(4)], axis=1)
        )
    table = jnp.concatenate(table, axis=0).astype(BF16)
    combo = jnp.transpose(combo[...].astype(F32)).astype(BF16)
    chips = owners // 2
    row = lax.broadcasted_iota(jnp.int32, (chips, owners), 0)
    col = lax.broadcasted_iota(jnp.int32, (chips, owners), 1)
    combo = dot(jnp.where(col == row * 2 + core, 1.0, 0.0).astype(BF16), combo)
    kind = lax.broadcasted_iota(jnp.int32, (chips, LANES), 1).astype(F32)
    for t in range(slots):
        hit = jnp.broadcast_to(combo[:, t : t + 1], kind.shape) == kind
        chosen[pl.ds(t, chips, stride=slots), :] = jnp.where(hit, 1.0, 0.0)
    chosen = chosen[:, : kinds * vectors].astype(BF16)
    picked = dot(chosen, table)
    for q in range(4):
        wide[pl.ds(q, chips * slots, stride=4), :] = picked[:, q * LANES : (q + 1) * LANES]
    out[...] = wide[...].astype(BF16)


def place_kernel(got, out, sems):
    places = [(got.at[:, t], out.at[t]) for t in range(out.shape[0])]
    for copy in fetch(places, sems):
        copy.wait()


VMEM = pl.BlockSpec(memory_space=pltpu.VMEM)
SMEM = pl.BlockSpec(memory_space=pltpu.SMEM)
HBM = pl.BlockSpec(memory_space=pltpu.HBM)


def in_hbm(x):
    return pltpu.with_memory_space_constraint(x, pltpu.HBM)


def params():
    return pltpu.CompilerParams(vmem_limit_bytes=32 * 1024 * 1024)


def per_device(kkr_matrix, kpoint_grid, lattice, delta_t, pair_count, pair_route, species):
    chips = lax.axis_size(CHIPS)
    cores = lax.axis_size(CORES)
    order = kkr_matrix.shape[2]
    kpoints = kkr_matrix.shape[0]
    vectors = lattice.shape[0]
    slots = pair_route.shape[1]
    kinds = delta_t.shape[0]
    scale = math.sqrt(order / (kpoints * chips * lax.axis_size("c")))
    chunk = 4 * kpoints + 2
    length = chips * chunk

    route, kind, count = pair_route.T, species.T, pair_count[None]
    outgoing, combo = pl.pallas_call(
        functools.partial(solve_kernel, kinds),
        out_shape=(
            jax.ShapeDtypeStruct((length, LANES), BF16),
            jax.ShapeDtypeStruct(route.shape, jnp.int32),
        ),
        in_specs=[HBM] * 6,
        out_specs=(VMEM, VMEM),
        scratch_shapes=[
            pltpu.SMEM((kpoints, 3), jnp.int32),
            pltpu.SMEM((3, vectors), jnp.int32),
            pltpu.VMEM(kkr_matrix.shape, BF16),
            pltpu.VMEM(route.shape, jnp.int32),
            pltpu.VMEM(kind.shape, jnp.int32),
            pltpu.VMEM(count.shape, jnp.int32),
            pltpu.VMEM((length, LANES), F32),
            pltpu.SemaphoreType.DMA((kpoints + 5,)),
        ],
        compiler_params=params(),
        name="solve",
    )(*map(in_hbm, (kpoint_grid, lattice.T, kkr_matrix, route, kind, count)))
    outgoing = outgoing.reshape(chips, chunk // 2, 2, LANES)
    arrived = lax.all_to_all(outgoing, CHIPS, split_axis=0, concat_axis=0, tiled=True)

    parts = pl.pallas_call(
        functools.partial(phase_kernel, kpoints, vectors),
        out_shape=jax.ShapeDtypeStruct((cores, vectors, 2 * order), BF16),
        in_specs=[VMEM],
        out_specs=VMEM,
        scratch_shapes=[pltpu.VMEM((length, LANES), F32)],
        compiler_params=params(),
        name="phase_sum",
    )(arrived.reshape(length, LANES))
    parts = lax.all_to_all(parts, CORES, split_axis=0, concat_axis=0, tiled=True)

    host_rows, sent = pl.pallas_call(
        functools.partial(product_kernel, scale),
        out_shape=(
            jax.ShapeDtypeStruct((2 * vectors, LANES), F32),
            jax.ShapeDtypeStruct((chips * slots * 4, LANES), BF16),
        ),
        in_specs=[VMEM, VMEM, VMEM],
        out_specs=(VMEM, VMEM),
        scratch_shapes=[
            pltpu.VMEM((chips * slots * 4, LANES), F32),
            pltpu.VMEM((4 * vectors, 2 * order), F32),
            pltpu.VMEM((chips * slots, LANES), F32),
        ],
        compiler_params=params(),
        name="product",
    )(parts, delta_t, combo)
    sent = sent.reshape(chips, slots * 4, LANES)
    got = lax.all_to_all(sent, CHIPS, split_axis=0, concat_axis=0, tiled=True)
    cluster = pl.pallas_call(
        place_kernel,
        out_shape=jax.ShapeDtypeStruct((slots, chips, 4, LANES), BF16),
        in_specs=[VMEM],
        out_specs=HBM,
        scratch_shapes=[pltpu.SemaphoreType.DMA((slots,))],
        compiler_params=params(),
        name="place",
    )(got.reshape(chips, slots, 4, LANES))
    return (host_rows, cluster.reshape(slots, order, LANES))


def solution(mesh):
    fine = Mesh(mesh.devices.reshape(8, 8, 2, 4), ("y", "z", "c", "pair"))
    ka = ("y", "z", "c")
    in_specs = (P(ka, None, None, None), P(ka, None), P(), P(), P(), P(), P())
    out_specs = (P(ka, "pair"), P(ka, None, "pair"))
    return jax.shard_map(
        per_device, mesh=fine, in_specs=in_specs, out_specs=out_specs, check_vma=False
    )
```
